256 devices in a mesh: dp: 32 (over y, x, core), mp: 8 (over z).
Axes of the slice: x: 4, y: 4, z: 8, core: 2. Of those that a mesh axis runs over, the one named last changes fastest.
Arguments:
- hidden: bfloat16 [16384, 18432], P('dp', 'mp'), may hold values from -6 to 6
- upstream: bfloat16 [16384, 2304], P('dp', 'mp'), may hold values from -1.5 to 1.5
- reward_head: float32 [2304], P('mp'), may hold values from -6 to 6
- margins: float32 [512], P('dp'), may hold values from -8 to 8
- ends: int32 [512, 2], P('dp'), may hold values from 0 to 511
- residual_error: bfloat16 [32, 18432, 2304], P('dp', 'mp'), may hold values from -24 to 24
- previous_q: float32 [2304, 32], replicated, may hold values from -6 to 6
Outputs:
- basis: float32 [18432, 32], P('mp')
- projection: float32 [2304, 32], replicated
The draws below stay inside these ranges and needn't reach their ends.
All inputs are finite; a program needn't handle non-finite values.
Results may differ from the reference program's by a relative error of at most 0.0017.
Values may be sent and summed in bfloat16 or wider, within the bound.
A program may use at most 128 MiB of HBM per device.

```python
import math
import jax
import jax.numpy as jnp
from jax import lax

D = 2304
FF = 18432
RANK = 32
TOK_DEV = 512
PAIRS = 16
TOKENS = 16384
N_DP = 32


def touch_ends(entries, own_key, low, largest):
    extent = entries.shape
    place = [jax.random.randint(jax.random.fold_in(own_key, axis), (), 0, extent[axis]) for axis in range(len(extent))]
    entries = entries.at[tuple(place)].set(low)
    longest = extent.index(max(extent))
    place[longest] = (place[longest] + 1) % extent[longest]
    return entries.at[tuple(place)].set(largest)


def shard_levels(rng, shape, shards, low, high):
    gain, own = 1.0, jax.random.fold_in(rng, 6)
    for dim, parts in shards:
        heights = jnp.exp(jax.random.uniform(jax.random.fold_in(own, dim), (parts,), jnp.float32, low / len(shards), high / len(shards)))
        gain = gain * jnp.repeat(heights, shape[dim] // parts).reshape([-1 if axis == dim else 1 for axis in range(len(shape))])
    return gain


def normal_values(rng, dims, spread, reach, pieces=(), held_as=jnp.bfloat16):
    array = spread * jax.random.normal(rng, dims, jnp.float32)
    if pieces:
        array = array * shard_levels(rng, dims, pieces, -0.22, 0.18)
    return jnp.clip(array, -reach, reach).astype(held_as)


def setup_inputs(seed: int = 0) -> dict:
    arg_keys = jax.random.split(jax.random.key(seed), 8)
    hidden = normal_values(arg_keys[0], (TOKENS, FF), 1.0, 6.0, ((0, 32), (1, 8)))
    upstream = normal_values(arg_keys[1], (TOKENS, D), 0.25, 1.5, ((0, 32), (1, 8)))
    reward_head = normal_values(arg_keys[2], (D,), 1.0, 6.0, ((0, 8),), jnp.float32)
    margins = normal_values(arg_keys[3], (TOKENS // 32,), 2.0, 8.0, ((0, 32),), jnp.float32)
    ends = touch_ends(jax.random.randint(arg_keys[4], (TOKENS // 32, 2), 0, TOK_DEV), jax.random.fold_in(arg_keys[4], 1), 0, TOK_DEV - 1).astype(jnp.int32)
    residual_error = normal_values(arg_keys[5], (N_DP, FF, D), 4.0, 24.0, ((0, 32), (1, 8)))
    previous_q = normal_values(arg_keys[6], (D, RANK), 1.0, 6.0, (), jnp.float32)
    return dict(hidden=hidden, upstream=upstream, reward_head=reward_head, margins=margins, ends=ends, residual_error=residual_error, previous_q=previous_q)


HI = lax.Precision.HIGHEST

def reference(hidden, upstream, reward_head, margins, ends, residual_error, previous_q):
    push = jax.nn.sigmoid(-margins)
    coef = jnp.stack([-push, push], axis=1).reshape(N_DP, PAIRS * 2)
    spots = ends.reshape(N_DP, PAIRS * 2)
    places = jnp.arange(TOK_DEV, dtype=jnp.int32)
    marks = (spots[:, :, None] == places[None, None, :]).astype(jnp.float32)
    token_weight = jnp.einsum('rpt,rp->rt', marks, coef, precision=HI).reshape(TOKENS)
    cotangent = (upstream.astype(jnp.float32) + token_weight[:, None] * reward_head[None, :]).astype(jnp.bfloat16)
    acts = hidden.reshape(N_DP, TOK_DEV, FF)
    cots = cotangent.reshape(N_DP, TOK_DEV, D)

    def left_term(items):
        act_rows, cot_rows, error = items
        probe = jnp.dot(cot_rows.astype(jnp.float32), previous_q, precision=HI)
        leading = jnp.dot(act_rows.astype(jnp.float32).T, probe, precision=HI)
        return leading + jnp.dot(error.astype(jnp.float32), previous_q, precision=HI)
    factor = lax.optimization_barrier(jnp.sum(lax.map(left_term, (acts, cots, residual_error)), axis=0))
    gram = jnp.dot(factor.T, factor, precision=HI)
    lower = jnp.linalg.cholesky(gram)
    ortho = lax.linalg.triangular_solve(lower, factor, left_side=False, lower=True, transpose_a=True)

    def right_term(items):
        act_rows, cot_rows, error = items
        weighted = jnp.dot(act_rows.astype(jnp.float32), ortho, precision=HI)
        leading = jnp.dot(cot_rows.astype(jnp.float32).T, weighted, precision=HI)
        return leading + jnp.dot(error.astype(jnp.float32).T, ortho, precision=HI)
    projection = lax.optimization_barrier(jnp.sum(lax.map(right_term, (acts, cots, residual_error)), axis=0)) / N_DP
    return (ortho * math.sqrt(FF), projection)
```

```python
import math

import jax
import jax.numpy as jnp
from jax import lax
from jax.experimental import pallas as pl
from jax.experimental.pallas import tpu as pltpu
from jax.sharding import PartitionSpec as P

FF = 18432
D = 2304
RANK = 32
TOK = 512
PAIRS = 16
WIDTH = 288
Z = 8
NDP = 32
OWNERS = 24
CH = 384
PARTS = 9
PART = D // PARTS
MESH = pl.DeviceIdType.MESH
HI = lax.Precision.HIGHEST
F32 = jnp.float32
BF16 = jnp.bfloat16


def ring(step, size):
    return min(step, size - step)


PLANE = sorted(
    ((dy, dx, dc) for dy in range(4) for dx in range(4) for dc in range(2) if (dy, dx, dc) != (0, 0, 0)),
    key=lambda o: -(ring(o[0], 4) + ring(o[1], 4)),
)
LINE = (4, 3, 5, 2, 6, 1, 7)


def split(x):
    high = x.astype(BF16)
    low = (x - high.astype(F32)).astype(BF16)
    return jnp.concatenate([high, low], axis=0)


def fold(x):
    half = x.shape[0] // 2
    return x[:half] + x[half:]


def mm(a, b):
    return lax.dot_general(a, b, (((1,), (0,)), ((), ())), preferred_element_type=F32)


def mm_t(a, b):
    return lax.dot_general(a, b, (((1,), (1,)), ((), ())), preferred_element_type=F32)


def column(row):
    n = row.shape[1]
    same = lax.broadcasted_iota(jnp.int32, (n, n), 0) == lax.broadcasted_iota(jnp.int32, (n, n), 1)
    return jnp.sum(jnp.where(same, jnp.broadcast_to(row, (n, n)), 0.0), axis=1, keepdims=True)


def inverse_lower(gram):
    rows = lax.broadcasted_iota(jnp.int32, (RANK, 128), 0)
    lanes = lax.broadcasted_iota(jnp.int32, (RANK, 128), 1)
    eye = (lanes == rows + RANK).astype(F32)
    m = jnp.concatenate([gram, jnp.zeros((RANK, 128 - RANK), F32)], axis=1) + eye
    for k in range(RANK - 1):
        col = m[:, k : k + 1]
        pivot = m[k : k + 1, :]
        scale = jnp.where(rows[:, :1] > k, col / m[k : k + 1, k : k + 1], 0.0)
        m = m - scale * pivot
    diag = jnp.sum(jnp.where(lanes == rows, m, 0.0), axis=1, keepdims=True)
    return (m * lax.rsqrt(diag))[:, RANK : 2 * RANK]


def kernel(
    hidden, upstream_t, head, margins, ends_t, error, q_t,
    basis_out, proj_out,
    h, e, u, hd, mg, en, q, q2, cot, c128,
    p_part, p_in, p_red, p_full,
    f_part, f_in, f_red, f_full,
    w_part, w_in, g_part, g_in,
    s_part, s_in, s_red, z_in, s_tot, s_full, b_out, r_out,
    load, e_load, out_sem,
    p_s, p_r, pg_s, pg_r, c_s, c_r, f_s, f_r, fg_s, fg_r,
    w_s, w_r, g_s, g_r, s_s, s_r, zs_s, zs_r, sg_s, sg_r,
):
    dp, z = lax.axis_index("dp"), lax.axis_index("mp")
    core, chip = lax.rem(dp, 2), lax.div(dp, 2)
    cy, cx = lax.div(chip, 4), lax.rem(chip, 4)

    def owns(y, x, c):
        return jnp.logical_or(c == 0, lax.rem(x + y, 2) == 0)

    def owned(y, x, c):
        place = y * 4 + x
        return jnp.where(c == 0, place, 16 + lax.div(place, 2))

    def chunk(ref, k):
        row = pl.multiple_of(lax.div(k, 6) * 8, 8)
        lane = pl.multiple_of(lax.rem(k, 6) * CH, 128)
        return ref.at[pl.ds(row, 8), pl.ds(lane, CH)]

    def away(o):
        dy, dx, dc = o
        return lax.rem(cy + dy, 4), lax.rem(cx + dx, 4), lax.rem(core + dc, 2)

    def along(step):
        return lax.rem(z + step, Z)

    is_owner, mine = owns(cy, cx, core), owned(cy, cx, core)

    def remote(src, dst, send, recv, **to):
        return pltpu.make_async_remote_copy(
            src_ref=src, dst_ref=dst, send_sem=send, recv_sem=recv, device_id=to, device_id_type=MESH
        )

    def arrived(ref, sem):
        pltpu.make_async_copy(ref, ref, sem).wait()

    loads = [
        pltpu.make_async_copy(src, dst, load.at[i])
        for i, (src, dst) in enumerate(
            [(upstream_t, u), (margins, mg), (ends_t, en), (head, hd), (q_t, q), (hidden, h)]
        )
    ]
    e_loads = [
        pltpu.make_async_copy(error.at[0, pl.ds(PART * i, PART)], e.at[pl.ds(PART * i, PART)], e_load.at[i])
        for i in range(PARTS)
    ]
    for c in loads[:5] + e_loads + loads[5:]:
        c.start()

    barrier = pltpu.get_barrier_semaphore()
    for o in PLANE:
        y, x, c = away(o)
        pl.semaphore_signal(barrier, inc=1, device_id={"dp": (y * 4 + x) * 2 + c}, device_id_type=MESH)
    for step in LINE:
        pl.semaphore_signal(barrier, inc=1, device_id={"mp": along(step)}, device_id_type=MESH)

    shift = pl.multiple_of(lax.rem(z, 4) * 32, 32)
    window = pl.multiple_of((2 * z + lax.div(z, 4)) * 128, 128)
    cot[...] = jnp.zeros_like(cot)
    for c in loads[:5]:
        c.wait()
    push = jax.nn.sigmoid(-column(mg[...]))
    spots = en[...].astype(F32)
    places = lax.broadcasted_iota(jnp.int32, (PAIRS, TOK), 1).astype(F32)
    weight = jnp.sum(
        jnp.where(places == column(spots[1:2]), push, 0.0) - jnp.where(places == column(spots[0:1]), push, 0.0),
        axis=0,
        keepdims=True,
    )
    direction = jnp.broadcast_to(hd[...], (128, WIDTH)).T[:, :1]
    cot[pl.ds(shift, WIDTH), :] = (u[...].astype(F32) + direction * weight).astype(BF16)
    q2[...] = split(q[...])
    p_part[...] = fold(mm(q2[:, pl.ds(window, CH)], cot[...]))
    pl.semaphore_wait(barrier, NDP - 1 + Z - 1)

    def p_chunk(ref, t):
        row = pl.multiple_of(lax.div(t, 2) * 8, 8)
        return ref.at[pl.ds(row, 8), pl.ds(pl.multiple_of(lax.rem(t, 2) * 256, 128), 256)]

    p_sends = [
        remote(p_chunk(p_part, along(o)), p_in.at[j], p_s.at[j], p_r, mp=along(o)) for j, o in enumerate(LINE)
    ]
    for c in p_sends:
        c.start()
    for i in range(PARTS):
        e_loads[i].wait()
        f_part[:, PART * i : PART * (i + 1)] = fold(mm_t(q2[...], e[PART * i : PART * (i + 1), :]))
    loads[5].wait()
    arrived(p_in, p_r)
    total = p_chunk(p_part, z)[...]
    for j in range(Z - 1):
        total += p_in[j]
    p_red[...] = total
    pg_sends = [remote(p_red, p_chunk(p_full, z), pg_s.at[j], pg_r, mp=along(o)) for j, o in enumerate(LINE)]
    for c in pg_sends:
        c.start()
    pltpu.make_async_copy(p_red, p_chunk(p_full, z), pg_r).start()

    def c_rows(ref):
        return ref.at[pl.ds(pl.multiple_of(z * WIDTH, 32), WIDTH)]

    def c_lanes(t):
        lane = pl.multiple_of(lax.div(t, 2) * 128, 128)
        return cot.at[pl.ds(shift, WIDTH), pl.ds(lane, 128)]

    c_sends = [
        remote(c_lanes(along(o)), c_rows(c128), c_s.at[j], c_r, mp=along(o)) for j, o in enumerate(LINE)
    ]
    for c in c_sends:
        c.start()
    pltpu.make_async_copy(c_lanes(z), c_rows(c128), c_r).start()
    for c in p_sends:
        c.wait_send()
    arrived(p_full, pg_r)
    f_part[...] += fold(mm(split(p_full[...]), h[...]))

    def to_owners(part, into, send, recv, start):
        for j, o in enumerate(PLANE):
            y, x, c = away(o)

            @pl.when(owns(y, x, c))
            def _(j=j, y=y, x=x, c=c):
                copy = remote(
                    chunk(part, owned(y, x, c)), into.at[j], send.at[j], recv, dp=(y * 4 + x) * 2 + c
                )
                if start:
                    copy.start()
                else:
                    copy.wait_send()

    def add_up(part, into, recv):
        arrived(into, recv)
        total = chunk(part, mine)[...]
        for j in range(NDP - 1):
            total += into[j]
        return total

    def hand_round(red, full, send, recv, start):
        for j, o in enumerate(PLANE):
            y, x, c = away(o)
            copy = remote(red, chunk(full, mine), send.at[j], recv, dp=(y * 4 + x) * 2 + c)
            if start:
                copy.start()
            else:
                copy.wait_send()

    to_owners(f_part, f_in, f_s, f_r, True)
    for c in pg_sends + c_sends:
        c.wait_send()

    @pl.when(is_owner)
    def _():
        f_red[...] = add_up(f_part, f_in, f_r)
        hand_round(f_red, f_full, fg_s, fg_r, True)
        pltpu.make_async_copy(f_red, chunk(f_full, mine), fg_r).start()

    to_owners(f_part, f_in, f_s, f_r, False)
    arrived(c128, c_r)
    arrived(f_full, fg_r)

    f2 = split(f_full[...])
    w_part[...] = fold(mm_t(f2, h[...]))

    def w_chunk(ref, t):
        row = pl.multiple_of(lax.rem(t, 2) * 16, 16)
        return ref.at[pl.ds(row, 16), pl.ds(pl.multiple_of(lax.div(t, 2) * 128, 128), 128)]

    w_sends = [
        remote(w_chunk(w_part, along(o)), w_in.at[j], w_s.at[j], w_r, mp=along(o)) for j, o in enumerate(LINE)
    ]
    for c in w_sends:
        c.start()
    gram = mm_t(f2, f2)
    g_part[...] = fold(gram[:, :RANK] + gram[:, RANK:])
    g_sends = [remote(g_part, g_in.at[z], g_s.at[j], g_r, mp=along(o)) for j, o in enumerate(LINE)]
    for c in g_sends:
        c.start()
    pltpu.make_async_copy(g_part, g_in.at[z], g_r).start()

    s_part[...] = fold(mm(f2, e[...]))

    @pl.when(is_owner)
    def _():
        hand_round(f_red, f_full, fg_s, fg_r, False)

    for c in w_sends + g_sends:
        c.wait_send()
    arrived(w_in, w_r)
    total = w_chunk(w_part, z)[...]
    for j in range(Z - 1):
        total += w_in[j]
    half = pl.ds(pl.multiple_of(lax.rem(z, 2) * 16, 16), 16)
    s_part[half, :] += fold(mm_t(split(total), c128[...]))

    to_owners(s_part, s_in, s_s, s_r, True)
    arrived(g_in, g_r)
    total = g_in[0]
    for j in range(1, Z):
        total += g_in[j]
    inverse = inverse_lower(total)

    @pl.when(is_owner)
    def _():
        s_red[...] = add_up(s_part, s_in, s_r)
        for j, o in enumerate(LINE):
            remote(s_red, z_in.at[z], zs_s.at[j], zs_r, mp=along(o)).start()
        pltpu.make_async_copy(s_red, z_in.at[z], zs_r).start()

    b_out[...] = jnp.dot(inverse * math.sqrt(FF), f_full[...], precision=HI, preferred_element_type=F32)
    out = pltpu.make_async_copy(b_out, basis_out, out_sem.at[0])
    out.start()

    @pl.when(is_owner)
    def _():
        arrived(z_in, zs_r)
        total = z_in[0]
        for j in range(1, Z):
            total += z_in[j]
        s_tot[...] = total
        hand_round(s_tot, s_full, sg_s, sg_r, True)
        pltpu.make_async_copy(s_tot, chunk(s_full, mine), sg_r).start()
        for j, o in enumerate(LINE):
            remote(s_red, z_in.at[z], zs_s.at[j], zs_r, mp=along(o)).wait_send()

    to_owners(s_part, s_in, s_s, s_r, False)
    arrived(s_full, sg_r)
    r_out[...] = jnp.dot(inverse * (1.0 / NDP), s_full[...], precision=HI, preferred_element_type=F32)
    last = pltpu.make_async_copy(r_out, proj_out, out_sem.at[1])
    last.start()

    @pl.when(is_owner)
    def _():
        hand_round(s_tot, s_full, sg_s, sg_r, False)

    out.wait()
    last.wait()


def shards(hidden, upstream, reward_head, margins, ends, residual_error, previous_q):
    any_spec = pl.BlockSpec(memory_space=pl.ANY)
    vmem, dma = pltpu.VMEM, pltpu.SemaphoreType.DMA
    whole = jax.ShapeDtypeStruct((RANK, D), F32)
    line, plane, one = dma((Z - 1,)), dma((NDP - 1,)), dma(())
    basis, projection = pl.pallas_call(
        kernel,
        out_shape=(whole, whole),
        in_specs=[any_spec] * 7,
        out_specs=(any_spec, any_spec),
        scratch_shapes=[
            vmem((TOK, D), BF16), vmem((D, D), BF16), vmem((WIDTH, TOK), BF16), vmem((1, WIDTH), F32),
            vmem((1, PAIRS), F32), vmem((2, PAIRS), jnp.int32), vmem((RANK, D), F32), vmem((2 * RANK, D), BF16),
            vmem((CH, TOK), BF16), vmem((D, 128), BF16),
            vmem((RANK, TOK), F32), vmem((Z - 1, 8, 256), F32), vmem((8, 256), F32), vmem((RANK, TOK), F32),
            vmem((RANK, D), F32), vmem((NDP - 1, 8, CH), F32), vmem((8, CH), F32), vmem((RANK, D), F32),
            vmem((RANK, TOK), F32), vmem((Z - 1, 16, 128), F32),
            vmem((RANK, RANK), F32), vmem((Z, RANK, RANK), F32),
            vmem((RANK, D), F32), vmem((NDP - 1, 8, CH), F32), vmem((8, CH), F32), vmem((Z, 8, CH), F32),
            vmem((8, CH), F32), vmem((RANK, D), F32), vmem((RANK, D), F32), vmem((RANK, D), F32),
            dma((6,)), dma((PARTS,)), dma((2,)),
            line, one, line, one, line, one, plane, one, plane, one,
            line, one, line, one, plane, one, line, one, plane, one,
        ],
        compiler_params=pltpu.CompilerParams(
            collective_id=0, has_side_effects=True, vmem_limit_bytes=48 * 1024 * 1024
        ),
        cost_estimate=pl.CostEstimate(flops=2_000_000_000, bytes_accessed=14_000_000, transcendentals=0),
        name="power_step",
    )(
        hidden, upstream.T, reward_head.reshape(1, WIDTH), margins.reshape(1, PAIRS), ends.T, residual_error,
        previous_q.T,
    )
    return basis.T, projection.T


def solution(mesh):
    in_specs = (
        P("dp", "mp"),
        P("dp", "mp"),
        P("mp"),
        P("dp"),
        P("dp", None),
        P("dp", "mp", None),
        P(),
    )
    out_specs = (P("mp", None), P())
    return jax.shard_map(shards, mesh=mesh, in_specs=in_specs, out_specs=out_specs, check_vma=False)
```

```python
import math

import jax
import jax.numpy as jnp
from jax import lax
from jax.experimental import pallas as pl
from jax.experimental.pallas import tpu as pltpu
from jax.sharding import PartitionSpec as P

FF = 18432
D = 2304
RANK = 32
TOK = 512
PAIRS = 16
WIDTH = 288
Z = 8
NDP = 32
GROUP = 4
CH = 384
PARTS = 9
PART = D // PARTS
MESH = pl.DeviceIdType.MESH
HI = lax.Precision.HIGHEST
F32 = jnp.float32
BF16 = jnp.bfloat16


def ring(step, size):
    return min(step, size - step)


PLANE = sorted(
    ((dy, dx, dc) for dy in range(4) for dx in range(4) for dc in range(2) if (dy, dx, dc) != (0, 0, 0)),
    key=lambda o: -(ring(o[0], 4) + ring(o[1], 4)),
)
LINE = (4, 3, 5, 2, 6, 1, 7)


def split(x):
    high = x.astype(BF16)
    low = (x - high.astype(F32)).astype(BF16)
    return jnp.concatenate([high, low], axis=0)


def fold(x):
    half = x.shape[0] // 2
    return x[:half] + x[half:]


def mm(a, b):
    return lax.dot_general(a, b, (((1,), (0,)), ((), ())), preferred_element_type=F32)


def mm_t(a, b):
    return lax.dot_general(a, b, (((1,), (1,)), ((), ())), preferred_element_type=F32)


def pack(x):
    return jnp.concatenate([x[8 * i : 8 * i + 8] for i in range(4)], axis=1)


def unpack(x):
    return jnp.concatenate([x[:, 32 * i : 32 * i + 32] for i in range(4)], axis=0)


def column(row):
    n = row.shape[1]
    same = lax.broadcasted_iota(jnp.int32, (n, n), 0) == lax.broadcasted_iota(jnp.int32, (n, n), 1)
    return jnp.sum(jnp.where(same, jnp.broadcast_to(row, (n, n)), 0.0), axis=1, keepdims=True)


def inverse_lower(gram):
    rows = lax.broadcasted_iota(jnp.int32, (RANK, 128), 0)
    lanes = lax.broadcasted_iota(jnp.int32, (RANK, 128), 1)
    eye = (lanes == rows + RANK).astype(F32)
    m = jnp.concatenate([gram, jnp.zeros((RANK, 128 - RANK), F32)], axis=1) + eye
    for k in range(RANK - 1):
        col = m[:, k : k + 1]
        pivot = m[k : k + 1, :]
        scale = jnp.where(rows[:, :1] > k, col / m[k : k + 1, k : k + 1], 0.0)
        m = m - scale * pivot
    diag = jnp.sum(jnp.where(lanes == rows, m, 0.0), axis=1, keepdims=True)
    return (m * lax.rsqrt(diag))[:, RANK : 2 * RANK]


def kernel(
    hidden, upstream_t, head, margins, ends_t, error, q_t,
    basis_out, proj_out,
    h, h_t, e, u, hd, mg, en, q, q2, cot, c128,
    p_part, p_in, p_red, p_full,
    f_part, f_in, f_red, f_full,
    w_part, w_in, g_part, g_in,
    s_part, s_in, s_red, z_in, s_tot, s_full,
    load, e_load,
    p_s, p_r, pg_s, pg_r, c_s, c_r, f_s, f_r, fg_s, fg_r,
    w_s, w_r, g_s, g_r, s_s, s_r, zs_s, zs_r, sg_s, sg_r,
):
    dp, z = lax.axis_index("dp"), lax.axis_index("mp")
    core, chip = lax.rem(dp, 2), lax.div(dp, 2)
    cy, cx = lax.div(chip, 4), lax.rem(chip, 4)

    def owns(y, x, c):
        return jnp.logical_or(c == 0, lax.rem(x + y, 2) == 0)

    def owned(y, x, c):
        place = y * 4 + x
        return jnp.where(c == 0, place, 16 + lax.div(place, 2))

    def chunk(ref, k):
        row = pl.multiple_of(lax.div(k, 6) * 8, 8)
        lane = pl.multiple_of(lax.rem(k, 6) * CH, 128)
        return ref.at[pl.ds(row, 8), pl.ds(lane, CH)]

    def away(o):
        dy, dx, dc = o
        return lax.rem(cy + dy, 4), lax.rem(cx + dx, 4), lax.rem(core + dc, 2)

    def along(step):
        return lax.rem(z + step, Z)

    is_owner, mine = owns(cy, cx, core), owned(cy, cx, core)

    def remote(src, dst, send, recv, **to):
        return pltpu.make_async_remote_copy(
            src_ref=src, dst_ref=dst, send_sem=send, recv_sem=recv, device_id=to, device_id_type=MESH
        )

    def arrived(ref, sem):
        pltpu.make_async_copy(ref, ref, sem).wait()

    loads = [
        pltpu.make_async_copy(src, dst, load.at[i])
        for i, (src, dst) in enumerate(
            [(upstream_t, u), (margins, mg), (ends_t, en), (head, hd), (q_t, q), (hidden, h)]
        )
    ]
    e_loads = [
        pltpu.make_async_copy(error.at[0, pl.ds(PART * i, PART)], e.at[pl.ds(PART * i, PART)], e_load.at[i])
        for i in range(PARTS)
    ]
    for c in loads[:5]:
        c.start()

    barrier = pltpu.get_barrier_semaphore()
    for step in LINE:
        pl.semaphore_signal(barrier, inc=1, device_id={"mp": along(step)}, device_id_type=MESH)
    for o in PLANE:
        y, x, c = away(o)
        pl.semaphore_signal(barrier, inc=1, device_id={"dp": (y * 4 + x) * 2 + c}, device_id_type=MESH)
    for c in e_loads + loads[5:]:
        c.start()

    shift = pl.multiple_of(lax.rem(z, 4) * 32, 32)
    window = pl.multiple_of((2 * z + lax.div(z, 4)) * 128, 128)
    cot[...] = jnp.zeros_like(cot)
    for c in loads[:5]:
        c.wait()
    push = jax.nn.sigmoid(-column(mg[...]))
    spots = en[...].astype(F32)
    places = lax.broadcasted_iota(jnp.int32, (PAIRS, TOK), 1).astype(F32)
    weight = jnp.sum(
        jnp.where(places == column(spots[1:2]), push, 0.0) - jnp.where(places == column(spots[0:1]), push, 0.0),
        axis=0,
        keepdims=True,
    )
    direction = jnp.broadcast_to(hd[...].reshape(1, WIDTH), (128, WIDTH)).T[:, :1]
    cot[pl.ds(shift, WIDTH), :] = (u[...].astype(F32) + direction * weight).astype(BF16)
    q2[...] = split(q[...])
    p_part[...] = fold(mm(q2[:, pl.ds(window, CH)], cot[...]))
    pl.semaphore_wait(barrier, NDP - 1 + Z - 1)

    def p_chunk(ref, t):
        row = pl.multiple_of(lax.div(t, 2) * 8, 8)
        return ref.at[pl.ds(row, 8), pl.ds(pl.multiple_of(lax.rem(t, 2) * 256, 128), 256)]

    p_sends = [
        remote(p_chunk(p_part, along(o)), p_in.at[j], p_s.at[j], p_r, mp=along(o)) for j, o in enumerate(LINE)
    ]
    for c in p_sends:
        c.start()
    def error_part(first, last):
        for i in range(first, last):
            e_loads[i].wait()
            f_part[:, PART * i : PART * (i + 1)] = fold(mm_t(q2[...], e[PART * i : PART * (i + 1), :]))

    error_part(0, 5)
    arrived(p_in, p_r)
    total = p_chunk(p_part, z)[...]
    for j in range(Z - 1):
        total += p_in[j]
    p_red[...] = total
    pg_sends = [remote(p_red, p_chunk(p_full, z), pg_s.at[j], pg_r, mp=along(o)) for j, o in enumerate(LINE)]
    for c in pg_sends:
        c.start()
    pltpu.make_async_copy(p_red, p_chunk(p_full, z), pg_r).start()

    def c_rows(ref):
        return ref.at[pl.ds(pl.multiple_of(z * WIDTH, 32), WIDTH)]

    def c_lanes(t):
        lane = pl.multiple_of(lax.rem(t, GROUP) * 128, 128)
        return cot.at[pl.ds(shift, WIDTH), pl.ds(lane, 128)]

    c_sends = [
        remote(c_lanes(along(o)), c_rows(c128), c_s.at[j], c_r, mp=along(o)) for j, o in enumerate(LINE)
    ]
    error_part(5, PARTS)
    loads[5].wait()
    for c in p_sends:
        c.wait_send()
    arrived(p_full, pg_r)
    f_part[...] += fold(mm(split(p_full[...]), h[...]))

    def to_owners(part, into, send, recv, start):
        for j, o in enumerate(PLANE):
            y, x, c = away(o)

            @pl.when(owns(y, x, c))
            def _(j=j, y=y, x=x, c=c):
                copy = remote(
                    chunk(part, owned(y, x, c)), into.at[j], send.at[j], recv, dp=(y * 4 + x) * 2 + c
                )
                if start:
                    copy.start()
                else:
                    copy.wait_send()

    def add_up(part, into, recv):
        arrived(into, recv)
        total = chunk(part, mine)[...]
        for j in range(NDP - 1):
            total += into[j]
        return total

    def hand_round(red, full, send, recv, start):
        for j, o in enumerate(PLANE):
            y, x, c = away(o)
            copy = remote(red, chunk(full, mine), send.at[j], recv, dp=(y * 4 + x) * 2 + c)
            if start:
                copy.start()
            else:
                copy.wait_send()

    to_owners(f_part, f_in, f_s, f_r, True)
    for c in c_sends:
        c.start()
    pltpu.make_async_copy(c_lanes(z), c_rows(c128), c_r).start()
    for c in pg_sends:
        c.wait_send()
    h_t[...] = h[...].T

    @pl.when(is_owner)
    def _():
        f_red[...] = add_up(f_part, f_in, f_r)
        hand_round(f_red, f_full, fg_s, fg_r, True)
        pltpu.make_async_copy(f_red, chunk(f_full, mine), fg_r).start()

    to_owners(f_part, f_in, f_s, f_r, False)
    arrived(f_full, fg_r)

    f2 = split(f_full[...])
    w_part[...] = fold(mm(f2, h_t[...]))

    def w_chunk(ref, t):
        return ref.at[:, pl.ds(pl.multiple_of(lax.rem(t, GROUP) * 128, 128), 128)]

    def near(step):
        return lax.div(z, GROUP) * GROUP + lax.rem(z + step, GROUP)

    w_sends = [
        remote(w_chunk(w_part, near(j + 1)), w_in.at[j], w_s.at[j], w_r, mp=near(j + 1)) for j in range(GROUP - 1)
    ]
    for c in w_sends:
        c.start()
    s_part[...] = fold(mm(f2, e[...]))
    arrived(c128, c_r)
    arrived(w_in, w_r)
    total = w_chunk(w_part, z)[...]
    for j in range(GROUP - 1):
        total += w_in[j]
    s_part[...] += fold(mm_t(split(total), c128[...]))
    to_owners(s_part, s_in, s_s, s_r, True)
    gram = mm_t(f2, f2)
    g_part[...] = pack(fold(gram[:, :RANK] + gram[:, RANK:]))
    g_sends = [remote(g_part, g_in.at[z], g_s.at[j], g_r, mp=along(o)) for j, o in enumerate(LINE)]
    for c in g_sends:
        c.start()
    pltpu.make_async_copy(g_part, g_in.at[z], g_r).start()

    for c in c_sends + w_sends + g_sends:
        c.wait_send()

    @pl.when(is_owner)
    def _():
        hand_round(f_red, f_full, fg_s, fg_r, False)

    @pl.when(is_owner)
    def _():
        s_red[...] = add_up(s_part, s_in, s_r)

        for j, o in enumerate(LINE):
            remote(s_red, z_in.at[z], zs_s.at[j], zs_r, mp=along(o)).start()
        pltpu.make_async_copy(s_red, z_in.at[z], zs_r).start()

    arrived(g_in, g_r)
    total = g_in[0]
    for j in range(1, Z):
        total += g_in[j]
    inverse = inverse_lower(unpack(total))

    basis_out[...] = jnp.dot(inverse * math.sqrt(FF), f_full[...], precision=HI, preferred_element_type=F32)

    @pl.when(is_owner)
    def _():
        arrived(z_in, zs_r)
        total = z_in[0]
        for j in range(1, Z):
            total += z_in[j]
        s_tot[...] = total
        hand_round(s_tot, s_full, sg_s, sg_r, True)
        pltpu.make_async_copy(s_tot, chunk(s_full, mine), sg_r).start()
        for j, o in enumerate(LINE):
            remote(s_red, z_in.at[z], zs_s.at[j], zs_r, mp=along(o)).wait_send()

    to_owners(s_part, s_in, s_s, s_r, False)
    arrived(s_full, sg_r)
    proj_out[...] = jnp.dot(inverse * (1.0 / NDP), s_full[...], precision=HI, preferred_element_type=F32)

    @pl.when(is_owner)
    def _():
        hand_round(s_tot, s_full, sg_s, sg_r, False)


def shards(hidden, upstream, reward_head, margins, ends, residual_error, previous_q):
    hbm_spec = pl.BlockSpec(memory_space=pltpu.HBM)
    vmem_spec = pl.BlockSpec(memory_space=pltpu.VMEM)
    vmem, dma = pltpu.VMEM, pltpu.SemaphoreType.DMA
    whole = vmem((RANK, D), F32)
    line, plane, few, one = dma((Z - 1,)), dma((NDP - 1,)), dma((GROUP - 1,)), dma(())
    basis, projection = pl.pallas_call(
        kernel,
        out_shape=(whole, whole),
        in_specs=[hbm_spec] * 7,
        out_specs=(vmem_spec, vmem_spec),
        scratch_shapes=[
            vmem((TOK, D), BF16), vmem((D, TOK), BF16), vmem((D, D), BF16), vmem((WIDTH, TOK), BF16), vmem((WIDTH,), F32),
            vmem((1, PAIRS), F32), vmem((2, PAIRS), jnp.int32), vmem((RANK, D), F32), vmem((2 * RANK, D), BF16),
            vmem((CH, TOK), BF16), vmem((D, 128), BF16),
            vmem((RANK, TOK), F32), vmem((Z - 1, 8, 256), F32), vmem((8, 256), F32), vmem((RANK, TOK), F32),
            vmem((RANK, D), F32), vmem((NDP - 1, 8, CH), F32), vmem((8, CH), F32), vmem((RANK, D), F32),
            vmem((RANK, TOK), F32), vmem((GROUP - 1, RANK, 128), F32),
            vmem((8, 128), F32), vmem((Z, 8, 128), F32),
            vmem((RANK, D), F32), vmem((NDP - 1, 8, CH), F32), vmem((8, CH), F32), vmem((Z, 8, CH), F32), vmem((8, CH), F32), vmem((RANK, D), F32),
            dma((6,)), dma((PARTS,)),
            line, one, line, one, line, one, plane, one, plane, one,
            few, one, line, one, plane, one, line, one, plane, one,
        ],
        compiler_params=pltpu.CompilerParams(
            collective_id=0, has_side_effects=True, vmem_limit_bytes=48 * 1024 * 1024
        ),
        cost_estimate=pl.CostEstimate(flops=2_000_000_000, bytes_accessed=14_000_000, transcendentals=0),
        name="power_step",
    )(
        *(
            pltpu.with_memory_space_constraint(x, pltpu.HBM)
            for x in (
                hidden, upstream.T, reward_head, margins.reshape(1, PAIRS), ends.T, residual_error, previous_q.T
            )
        )
    )
    return basis.T, projection.T


def solution(mesh):
    in_specs = (
        P("dp", "mp"),
        P("dp", "mp"),
        P("mp"),
        P("dp"),
        P("dp", None),
        P("dp", "mp", None),
        P(),
    )
    out_specs = (P("mp", None), P())
    return jax.shard_map(shards, mesh=mesh, in_specs=in_specs, out_specs=out_specs, check_vma=False)
```

```python
import math

import jax
import jax.numpy as jnp
from jax import lax
from jax.experimental import pallas as pl
from jax.experimental.pallas import tpu as pltpu
from jax.sharding import PartitionSpec as P

FF = 18432
D = 2304
RANK = 32
TOK = 512
PAIRS = 16
WIDTH = 288
Z = 8
NDP = 32
GROUP = 4
OWNERS = 24
CH = 384
PARTS = 9
PART = D // PARTS
MESH = pl.DeviceIdType.MESH
F32 = jnp.float32
BF16 = jnp.bfloat16


def ring(step, size):
    return min(step, size - step)


PLANE = sorted(
    ((dy, dx, dc) for dy in range(4) for dx in range(4) for dc in range(2) if (dy, dx, dc) != (0, 0, 0)),
    key=lambda o: -(ring(o[0], 4) + ring(o[1], 4)),
)
LINE = (4, 3, 5, 2, 6, 1, 7)


def split(x):
    high = x.astype(BF16)
    low = (x - high.astype(F32)).astype(BF16)
    return jnp.concatenate([high, low], axis=0)


def fold(x):
    half = x.shape[0] // 2
    return x[:half] + x[half:]


def mm(a, b):
    return lax.dot_general(a, b, (((1,), (0,)), ((), ())), preferred_element_type=F32)


def mm_t(a, b):
    return lax.dot_general(a, b, (((1,), (1,)), ((), ())), preferred_element_type=F32)


def pack(x):
    return jnp.concatenate([x[8 * i : 8 * i + 8] for i in range(4)], axis=1)


def unpack(x):
    return jnp.concatenate([x[:, 32 * i : 32 * i + 32] for i in range(4)], axis=0)


def thirds(x):
    high = x.astype(BF16).astype(F32)
    middle = (x - high).astype(BF16).astype(F32)
    return high, middle, (x - high - middle).astype(BF16).astype(F32)


def left_terms(x):
    high, middle, low = thirds(x)
    return jnp.concatenate([high, high, middle, high, middle, low], axis=1).astype(BF16)


def right_terms(x):
    high, middle, low = (t.astype(BF16) for t in thirds(x))
    return jnp.concatenate([high, middle, high, low, middle, high], axis=0)


def column(row):
    n = row.shape[1]
    same = lax.broadcasted_iota(jnp.int32, (n, n), 0) == lax.broadcasted_iota(jnp.int32, (n, n), 1)
    return jnp.sum(jnp.where(same, jnp.broadcast_to(row, (n, n)), 0.0), axis=1, keepdims=True)


def inverse_lower(gram):
    rows = lax.broadcasted_iota(jnp.int32, (RANK, 128), 0)
    lanes = lax.broadcasted_iota(jnp.int32, (RANK, 128), 1)
    eye = (lanes == rows + RANK).astype(F32)
    m = jnp.concatenate([gram, jnp.zeros((RANK, 128 - RANK), F32)], axis=1) + eye
    for k in range(RANK - 1):
        col = m[:, k : k + 1]
        pivot = m[k : k + 1, :]
        scale = jnp.where(rows[:, :1] > k, col / m[k : k + 1, k : k + 1], 0.0)
        m = m - scale * pivot
    diag = jnp.sum(jnp.where(lanes == rows, m, 0.0), axis=1, keepdims=True)
    return (m * lax.rsqrt(diag))[:, RANK : 2 * RANK]


def kernel(
    hidden, upstream_t, head, margins, ends_t, error, q_t,
    both,
    h, h_t, e, u, hd, mg, en, q, q2, cot, c128,
    p_part, p_in, p_red, p_full,
    f_part, f_in, f_red, f_full,
    w_part, w_in, g_part, g_in,
    s_part, s_in, s_red, z_in, s_tot, s_full,
    load, e_load,
    p_s, p_r, pg_s, pg_r, c_s, c_r, f_s, f_r, fg_s, fg_r,
    w_s, w_r, g_s, g_r, s_s, s_r, zs_s, zs_r, sg_s, sg_r,
):
    dp, z = lax.axis_index("dp"), lax.axis_index("mp")
    core, chip = lax.rem(dp, 2), lax.div(dp, 2)
    cy, cx = lax.div(chip, 4), lax.rem(chip, 4)

    def owns(y, x, c):
        return jnp.logical_or(c == 0, lax.rem(x + y, 2) == 0)

    def owned(y, x, c):
        place = y * 4 + x
        return jnp.where(c == 0, place, 16 + lax.div(place, 2))

    def chunk(ref, k):
        row = pl.multiple_of(lax.div(k, 6) * 8, 8)
        lane = pl.multiple_of(lax.rem(k, 6) * CH, 128)
        return ref.at[pl.ds(row, 8), pl.ds(lane, CH)]

    def away(o):
        dy, dx, dc = o
        return lax.rem(cy + dy, 4), lax.rem(cx + dx, 4), lax.rem(core + dc, 2)

    def along(step):
        return lax.rem(z + step, Z)

    is_owner, mine = owns(cy, cx, core), owned(cy, cx, core)

    def remote(src, dst, send, recv, **to):
        return pltpu.make_async_remote_copy(
            src_ref=src, dst_ref=dst, send_sem=send, recv_sem=recv, device_id=to, device_id_type=MESH
        )

    def arrived(ref, sem):
        pltpu.make_async_copy(ref, ref, sem).wait()

    loads = [
        pltpu.make_async_copy(src, dst, load.at[i])
        for i, (src, dst) in enumerate(
            [(upstream_t, u), (margins, mg), (ends_t, en), (head, hd), (q_t, q), (hidden, h)]
        )
    ]
    e_loads = [
        pltpu.make_async_copy(error.at[0, pl.ds(PART * i, PART)], e.at[pl.ds(PART * i, PART)], e_load.at[i])
        for i in range(PARTS)
    ]
    for c in loads[:5]:
        c.start()

    barrier = pltpu.get_barrier_semaphore()
    for step in LINE:
        pl.semaphore_signal(barrier, inc=1, device_id={"mp": along(step)}, device_id_type=MESH)
    for o in PLANE:
        y, x, c = away(o)
        pl.semaphore_signal(barrier, inc=1, device_id={"dp": (y * 4 + x) * 2 + c}, device_id_type=MESH)
    for c in e_loads + loads[5:]:
        c.start()

    shift = pl.multiple_of(lax.rem(z, 4) * 32, 32)
    window = pl.multiple_of((2 * z + lax.div(z, 4)) * 128, 128)
    cot[...] = jnp.zeros_like(cot)
    for c in loads[:5]:
        c.wait()
    push = jax.nn.sigmoid(-column(mg[...]))
    spots = en[...].astype(F32)
    places = lax.broadcasted_iota(jnp.int32, (PAIRS, TOK), 1).astype(F32)
    weight = jnp.sum(
        jnp.where(places == column(spots[1:2]), push, 0.0) - jnp.where(places == column(spots[0:1]), push, 0.0),
        axis=0,
        keepdims=True,
    )
    direction = jnp.broadcast_to(hd[...].reshape(1, WIDTH), (128, WIDTH)).T[:, :1]
    cot[pl.ds(shift, WIDTH), :] = (u[...].astype(F32) + direction * weight).astype(BF16)
    q2[...] = split(q[...])
    p_part[...] = fold(mm(q2[:, pl.ds(window, CH)], cot[...]))
    pl.semaphore_wait(barrier, NDP - 1 + Z - 1)

    def p_chunk(ref, t):
        row = pl.multiple_of(lax.div(t, 2) * 8, 8)
        return ref.at[pl.ds(row, 8), pl.ds(pl.multiple_of(lax.rem(t, 2) * 256, 128), 256)]

    p_sends = [
        remote(p_chunk(p_part, along(o)), p_in.at[j], p_s, p_r, mp=along(o)) for j, o in enumerate(LINE)
    ]
    for c in p_sends:
        c.start()
    def error_part(first, last):
        for i in range(first, last):
            e_loads[i].wait()
            f_part[:, PART * i : PART * (i + 1)] = fold(mm_t(q2[...], e[PART * i : PART * (i + 1), :]))

    error_part(0, 5)
    arrived(p_in, p_r)
    total = p_chunk(p_part, z)[...]
    for j in range(Z - 1):
        total += p_in[j]
    p_red[...] = total
    pg_sends = [remote(p_red, p_chunk(p_full, z), pg_s, pg_r, mp=along(o)) for j, o in enumerate(LINE)]
    for c in pg_sends:
        c.start()
    pltpu.make_async_copy(p_red, p_chunk(p_full, z), pg_r).start()

    def c_rows(ref):
        return ref.at[pl.ds(pl.multiple_of(z * WIDTH, 32), WIDTH)]

    def c_lanes(t):
        lane = pl.multiple_of(lax.rem(t, GROUP) * 128, 128)
        return cot.at[pl.ds(shift, WIDTH), pl.ds(lane, 128)]

    c_sends = [
        remote(c_lanes(along(o)), c_rows(c128), c_s, c_r, mp=along(o)) for j, o in enumerate(LINE)
    ]
    error_part(5, PARTS)
    loads[5].wait()
    arrived(p_in, p_s)
    arrived(p_full, pg_r)
    f_part[...] += fold(mm(split(p_full[...]), h[...]))

    def to_owners(part, into, send, recv):
        for j, o in enumerate(PLANE):
            y, x, c = away(o)

            @pl.when(owns(y, x, c))
            def _(j=j, y=y, x=x, c=c):
                remote(chunk(part, owned(y, x, c)), into.at[j], send, recv, dp=(y * 4 + x) * 2 + c).start()

    def sent(into, send):
        @pl.when(is_owner)
        def _():
            arrived(into.at[pl.ds(0, OWNERS - 1)], send)

        @pl.when(jnp.logical_not(is_owner))
        def _():
            arrived(into.at[pl.ds(0, OWNERS)], send)

    def add_up(part, into, recv):
        arrived(into, recv)
        total = chunk(part, mine)[...]
        for j in range(NDP - 1):
            total += into[j]
        return total

    def hand_round(red, full, send, recv):
        for o in PLANE:
            y, x, c = away(o)
            remote(red, chunk(full, mine), send, recv, dp=(y * 4 + x) * 2 + c).start()
        pltpu.make_async_copy(red, chunk(full, mine), recv).start()

    to_owners(f_part, f_in, f_s, f_r)
    for c in c_sends:
        c.start()
    pltpu.make_async_copy(c_lanes(z), c_rows(c128), c_r).start()
    arrived(p_in, pg_s)
    h_t[...] = h[...].T

    @pl.when(is_owner)
    def _():
        f_red[...] = add_up(f_part, f_in, f_r)
        hand_round(f_red, f_full, fg_s, fg_r)

    sent(f_in, f_s)
    arrived(f_full, fg_r)

    f2 = split(f_full[...])
    w_part[...] = fold(mm(f2, h_t[...]))

    def w_chunk(ref, t):
        return ref.at[:, pl.ds(pl.multiple_of(lax.rem(t, GROUP) * 128, 128), 128)]

    def near(step):
        return lax.div(z, GROUP) * GROUP + lax.rem(z + step, GROUP)

    w_sends = [
        remote(w_chunk(w_part, near(j + 1)), w_in.at[j], w_s, w_r, mp=near(j + 1)) for j in range(GROUP - 1)
    ]
    for c in w_sends:
        c.start()
    s_part[...] = fold(mm(f2, e[...]))
    arrived(c128, c_r)
    arrived(w_in, w_r)
    total = w_chunk(w_part, z)[...]
    for j in range(GROUP - 1):
        total += w_in[j]
    s_part[...] += fold(mm_t(split(total), c128[...]))
    to_owners(s_part, s_in, s_s, s_r)
    gram = mm_t(f2, f2)
    g_part[...] = pack(fold(gram[:, :RANK] + gram[:, RANK:]))
    g_sends = [remote(g_part, g_in.at[z], g_s, g_r, mp=along(o)) for j, o in enumerate(LINE)]
    for c in g_sends:
        c.start()
    pltpu.make_async_copy(g_part, g_in.at[z], g_r).start()

    arrived(c128.at[pl.ds(0, 7 * WIDTH)], c_s)
    arrived(w_in, w_s)
    arrived(g_in.at[pl.ds(0, Z - 1)], g_s)

    @pl.when(is_owner)
    def _():
        arrived(f_in, fg_s)

    @pl.when(is_owner)
    def _():
        s_red[...] = add_up(s_part, s_in, s_r)

        for j, o in enumerate(LINE):
            remote(s_red, z_in.at[z], zs_s, zs_r, mp=along(o)).start()
        pltpu.make_async_copy(s_red, z_in.at[z], zs_r).start()

    arrived(g_in, g_r)
    total = g_in[0]
    for j in range(1, Z):
        total += g_in[j]
    inverse = inverse_lower(unpack(total))

    left = left_terms(inverse)
    both[:RANK] = mm(left, right_terms(f_full[...]))

    @pl.when(is_owner)
    def _():
        arrived(z_in, zs_r)
        total = z_in[0]
        for j in range(1, Z):
            total += z_in[j]
        s_tot[...] = total
        hand_round(s_tot, s_full, sg_s, sg_r)
        arrived(z_in.at[pl.ds(0, Z - 1)], zs_s)

    sent(s_in, s_s)
    arrived(s_full, sg_r)
    both[RANK:] = mm(left, right_terms(s_full[...]))

    @pl.when(is_owner)
    def _():
        arrived(s_in, sg_s)


def shards(hidden, upstream, reward_head, margins, ends, residual_error, previous_q):
    hbm_spec = pl.BlockSpec(memory_space=pltpu.HBM)
    vmem_spec = pl.BlockSpec(memory_space=pltpu.VMEM)
    vmem, dma = pltpu.VMEM, pltpu.SemaphoreType.DMA
    both = pl.pallas_call(
        kernel,
        out_shape=vmem((2 * RANK, D), F32),
        in_specs=[hbm_spec] * 7,
        out_specs=vmem_spec,
        scratch_shapes=[
            vmem((TOK, D), BF16), vmem((D, TOK), BF16), vmem((D, D), BF16), vmem((WIDTH, TOK), BF16), vmem((WIDTH,), F32),
            vmem((1, PAIRS), F32), vmem((2, PAIRS), jnp.int32), vmem((RANK, D), F32), vmem((2 * RANK, D), BF16),
            vmem((CH, TOK), BF16), vmem((D, 128), BF16),
            vmem((RANK, TOK), F32), vmem((Z - 1, 8, 256), F32), vmem((8, 256), F32), vmem((RANK, TOK), F32),
            vmem((RANK, D), F32), vmem((NDP - 1, 8, CH), F32), vmem((8, CH), F32), vmem((RANK, D), F32),
            vmem((RANK, TOK), F32), vmem((GROUP - 1, RANK, 128), F32),
            vmem((8, 128), F32), vmem((Z, 8, 128), F32),
            vmem((RANK, D), F32), vmem((NDP - 1, 8, CH), F32), vmem((8, CH), F32), vmem((Z, 8, CH), F32), vmem((8, CH), F32), vmem((RANK, D), F32),
            dma((6,)), dma((PARTS,)),
            *[dma(())] * 20,
        ],
        compiler_params=pltpu.CompilerParams(
            collective_id=0, has_side_effects=True, vmem_limit_bytes=48 * 1024 * 1024
        ),
        cost_estimate=pl.CostEstimate(flops=2_000_000_000, bytes_accessed=14_000_000, transcendentals=0),
        name="power_step",
    )(
        *(
            pltpu.with_memory_space_constraint(x, pltpu.HBM)
            for x in (
                hidden, upstream.T, reward_head, margins.reshape(1, PAIRS), ends.T, residual_error, previous_q.T
            )
        )
    )
    return both[:RANK].T * math.sqrt(FF), both[RANK:].T * (1.0 / NDP)


def solution(mesh):
    in_specs = (
        P("dp", "mp"),
        P("dp", "mp"),
        P("mp"),
        P("dp"),
        P("dp", None),
        P("dp", "mp", None),
        P(),
    )
    out_specs = (P("mp", None), P())
    return jax.shard_map(shards, mesh=mesh, in_specs=in_specs, out_specs=out_specs, check_vma=False)
```

```python
import math

import jax
import jax.numpy as jnp
from jax import lax
from jax.experimental import pallas as pl
from jax.experimental.pallas import tpu as pltpu
from jax.sharding import PartitionSpec as P

FF = 18432
D = 2304
RANK = 32
TOK = 512
PAIRS = 16
WIDTH = 288
Z = 8
NDP = 32
HALF = WIDTH // 2
OWNERS = 24
CH = 384
PARTS = 9
PART = D // PARTS
MESH = pl.DeviceIdType.MESH
F32 = jnp.float32
BF16 = jnp.bfloat16


def ring(step, size):
    return min(step, size - step)


PLANE = sorted(
    ((dy, dx, dc) for dy in range(4) for dx in range(4) for dc in range(2) if (dy, dx, dc) != (0, 0, 0)),
    key=lambda o: -(ring(o[0], 4) + ring(o[1], 4)),
)
CHIPS = [o[:2] for o in PLANE if o[2] == 0]
LINE = (4, 3, 5, 2, 6, 1, 7)


def split(x):
    high = x.astype(BF16)
    low = (x - high.astype(F32)).astype(BF16)
    return jnp.concatenate([high, low], axis=0)


def fold(x):
    half = x.shape[0] // 2
    return x[:half] + x[half:]


def mm(a, b):
    return lax.dot_general(a, b, (((1,), (0,)), ((), ())), preferred_element_type=F32)


def mm_t(a, b):
    return lax.dot_general(a, b, (((1,), (1,)), ((), ())), preferred_element_type=F32)


def pack(x):
    return jnp.concatenate([x[8 * i : 8 * i + 8] for i in range(4)], axis=1)


def unpack(x):
    return jnp.concatenate([x[:, 32 * i : 32 * i + 32] for i in range(4)], axis=0)


def thirds(x):
    high = x.astype(BF16).astype(F32)
    middle = (x - high).astype(BF16).astype(F32)
    return high, middle, (x - high - middle).astype(BF16).astype(F32)


def left_terms(x):
    high, middle, low = thirds(x)
    return jnp.concatenate([high, high, middle, high, middle, low], axis=1).astype(BF16)


def right_terms(x):
    high, middle, low = (t.astype(BF16) for t in thirds(x))
    return jnp.concatenate([high, middle, high, low, middle, high], axis=0)


def interleave(a, b):
    low = lax.broadcasted_iota(jnp.int32, a.shape, 1) < 64
    return jnp.where(low, a, pltpu.roll(b, 64, 1)), jnp.where(low, pltpu.roll(a, 64, 1), b)


def column(row):
    n = row.shape[1]
    same = lax.broadcasted_iota(jnp.int32, (n, n), 0) == lax.broadcasted_iota(jnp.int32, (n, n), 1)
    return jnp.sum(jnp.where(same, jnp.broadcast_to(row, (n, n)), 0.0), axis=1, keepdims=True)


def inverse_lower(gram):
    rows = lax.broadcasted_iota(jnp.int32, (RANK, 128), 0)
    lanes = lax.broadcasted_iota(jnp.int32, (RANK, 128), 1)
    eye = (lanes == rows + RANK).astype(F32)
    m = jnp.concatenate([gram, jnp.zeros((RANK, 128 - RANK), F32)], axis=1) + eye
    for k in range(RANK - 1):
        col = m[:, k : k + 1]
        pivot = m[k : k + 1, :]
        scale = jnp.where(rows[:, :1] > k, col / m[k : k + 1, k : k + 1], 0.0)
        m = m - scale * pivot
    diag = jnp.sum(jnp.where(lanes == rows, m, 0.0), axis=1, keepdims=True)
    return (m * lax.rsqrt(diag))[:, RANK : 2 * RANK]


def kernel(
    hidden, upstream_t, head, margins, ends_t, error, q_t,
    both,
    h, h_t, e, u, hd, mg, en, q, q2, cot, cot_x, c_pack, c_all,
    p_part, p_in, p_red, p_full,
    f_part, f_other, f_in, f_red, f_full,
    w_part, w_pack, w_in, g_part, g_in,
    s_part, s_other, s_in, s_red, z_in, s_tot, s_full,
    load, e_load,
    p_s, p_r, pg_s, pg_r, c_s, c_r, f_s, f_r, fg_s, fg_r,
    w_s, w_r, g_s, g_r, s_s, s_r, zs_s, zs_r, sg_s, sg_r,
    hx_s, hx_r, fx_s, fx_r, cx_s, cx_r, cf_s, cf_r, sx_s, sx_r,
):
    dp, z = lax.axis_index("dp"), lax.axis_index("mp")
    core, chip = lax.rem(dp, 2), lax.div(dp, 2)
    cy, cx = lax.div(chip, 4), lax.rem(chip, 4)

    def place(y, x):
        return lax.rem(x + y + 2 * core, 4)

    def chunk(ref, y, x):
        k = 3 * y + place(y, x) - 1
        row = pl.multiple_of(16 * core + lax.div(k, 6) * 8, 8)
        lane = pl.multiple_of(lax.rem(k, 6) * CH, 128)
        return ref.at[pl.ds(row, 8), pl.ds(lane, CH)]

    def away(o):
        dy, dx, dc = o
        return lax.rem(cy + dy, 4), lax.rem(cx + dx, 4), lax.rem(core + dc, 2)

    def along(step):
        return lax.rem(z + step, Z)

    is_owner = place(cy, cx) != 0
    own_half = pl.ds(pl.multiple_of(16 * core, 16), 16)
    other_half = pl.ds(pl.multiple_of(16 * (1 - core), 16), 16)
    sibling = dp + 1 - 2 * core

    def remote(src, dst, send, recv, **to):
        return pltpu.make_async_remote_copy(
            src_ref=src, dst_ref=dst, send_sem=send, recv_sem=recv, device_id=to, device_id_type=MESH
        )

    def arrived(ref, sem):
        pltpu.make_async_copy(ref, ref, sem).wait()

    loads = [
        pltpu.make_async_copy(src, dst, load.at[i])
        for i, (src, dst) in enumerate(
            [(upstream_t, u), (margins, mg), (ends_t, en), (head, hd), (q_t, q), (hidden, h.at[pl.ds(0, TOK)])]
        )
    ]
    e_loads = [
        pltpu.make_async_copy(error.at[0, pl.ds(PART * i, PART)], e.at[pl.ds(PART * i, PART)], e_load.at[i])
        for i in range(PARTS)
    ]
    for c in loads[:5]:
        c.start()

    barrier = pltpu.get_barrier_semaphore()
    for step in LINE:
        pl.semaphore_signal(barrier, inc=1, device_id={"mp": along(step)}, device_id_type=MESH)
        pl.semaphore_signal(barrier, inc=1, device_id={"dp": sibling, "mp": along(step)}, device_id_type=MESH)
    for o in PLANE:
        y, x, c = away(o)
        pl.semaphore_signal(barrier, inc=1, device_id={"dp": (y * 4 + x) * 2 + c}, device_id_type=MESH)
    for c in e_loads + loads[5:]:
        c.start()

    shift = pl.multiple_of(lax.rem(z, 4) * 32, 32)
    window = pl.multiple_of((2 * z + lax.div(z, 4)) * 128, 128)
    cot[...] = jnp.zeros_like(cot)
    for c in loads[:5]:
        c.wait()
    push = jax.nn.sigmoid(-column(mg[...]))
    spots = en[...].astype(F32)
    places = lax.broadcasted_iota(jnp.int32, (PAIRS, TOK), 1).astype(F32)
    weight = jnp.sum(
        jnp.where(places == column(spots[1:2]), push, 0.0) - jnp.where(places == column(spots[0:1]), push, 0.0),
        axis=0,
        keepdims=True,
    )
    direction = jnp.broadcast_to(hd[...].reshape(1, WIDTH), (128, WIDTH)).T[:, :1]
    cot[pl.ds(shift, WIDTH), :] = (u[...].astype(F32) + direction * weight).astype(BF16)
    q2[...] = split(q[...])
    p_part[...] = fold(mm(q2[:, pl.ds(window, CH)], cot[...]))
    pl.semaphore_wait(barrier, NDP - 1 + 2 * (Z - 1))

    def replicas(mine, other):
        return jnp.where(core == 0, mine, other), jnp.where(core == 0, other, mine)

    def p_chunk(ref, t):
        row = pl.multiple_of(lax.div(t, 2) * 8, 8)
        return ref.at[pl.ds(row, 8), pl.ds(pl.multiple_of(lax.rem(t, 2) * 256, 128), 256)]

    p_sends = [
        remote(p_chunk(p_part, along(o)), p_in.at[j], p_s, p_r, mp=along(o)) for j, o in enumerate(LINE)
    ]
    for c in p_sends:
        c.start()
    def c_half(c):
        return cot.at[pl.ds(pl.multiple_of(shift + HALF * c, 16), HALF), :]

    remote(c_half(1 - core), cot_x, cx_s, cx_r, dp=sibling).start()
    remote(hidden, h.at[pl.ds(TOK, TOK)], hx_s, hx_r, dp=sibling).start()
    def error_part(first, last):
        for i in range(first, last):
            e_loads[i].wait()
            f_part[:, PART * i : PART * (i + 1)] = fold(mm_t(q2[...], e[PART * i : PART * (i + 1), :]))

    error_part(0, 5)
    arrived(p_in, p_r)
    total = p_chunk(p_part, z)[...]
    for j in range(Z - 1):
        total += p_in[j]
    p_red[...] = total
    def p_place(slot):
        row = pl.multiple_of(lax.rem(lax.div(z, 2), 2) * 8, 8)
        return p_full.at[slot, pl.ds(row, 8), pl.ds(pl.multiple_of(lax.rem(z, 2) * 256, 128), 256)]

    stays = lax.div(z, 4) == core

    @pl.when(stays)
    def _():
        for o in LINE:
            remote(p_red, p_place(0), pg_s, pg_r, mp=along(o)).start()
        pltpu.make_async_copy(p_red, p_place(0), pg_r).start()

    @pl.when(jnp.logical_not(stays))
    def _():
        for o in LINE:
            remote(p_red, p_place(1), pg_s, pg_r, dp=sibling, mp=along(o)).start()
        remote(p_red, p_place(1), pg_s, pg_r, dp=sibling).start()

    def c_rows(t, c):
        return c_all.at[pl.ds(pl.multiple_of(t * WIDTH + c * HALF, 16), HALF)]

    error_part(5, PARTS)
    remote(f_part.at[other_half, :], f_other, fx_s, fx_r, dp=sibling).start()
    arrived(cot_x, cx_r)
    first, second = replicas(c_half(core)[...].astype(F32), cot_x[...].astype(F32))
    for t in range(4):
        even, odd = interleave(first[:, 128 * t : 128 * t + 128], second[:, 128 * t : 128 * t + 128])
        c_pack[2 * t] = even.astype(BF16)
        c_pack[2 * t + 1] = odd.astype(BF16)
    loads[5].wait()
    arrived(p_in, p_s)
    arrived(h.at[pl.ds(TOK, TOK)], hx_r)
    arrived(f_other, fx_r)
    arrived(p_full, pg_r)
    probe = jnp.concatenate([p_full[0], p_full[1]], axis=1)
    f_part[own_half, :] += f_other[...] + fold(mm(split(probe), h[...]))

    def to_owners(part, into, send, recv):
        for j, (dy, dx) in enumerate(CHIPS):
            y, x = lax.rem(cy + dy, 4), lax.rem(cx + dx, 4)

            @pl.when(place(y, x) != 0)
            def _(j=j, y=y, x=x):
                remote(chunk(part, y, x), into.at[j], send, recv, dp=y * 8 + x * 2 + core).start()

    def sent(into, send):
        @pl.when(is_owner)
        def _():
            arrived(into.at[pl.ds(0, OWNERS // 2 - 1)], send)

        @pl.when(jnp.logical_not(is_owner))
        def _():
            arrived(into.at[pl.ds(0, OWNERS // 2)], send)

    def add_up(part, into, recv):
        arrived(into, recv)
        total = chunk(part, cy, cx)[...]
        for j in range(len(CHIPS)):
            total += into[j]
        return total

    def hand_round(red, full, send, recv):
        for o in PLANE:
            y, x, c = away(o)
            remote(red, chunk(full, cy, cx), send, recv, dp=(y * 4 + x) * 2 + c).start()
        pltpu.make_async_copy(red, chunk(full, cy, cx), recv).start()

    to_owners(f_part, f_in, f_s, f_r)
    for o in LINE:
        remote(c_pack.at[along(o)], c_rows(z, core), c_s, c_r, mp=along(o)).start()
    pltpu.make_async_copy(c_pack.at[z], c_rows(z, core), c_r).start()
    @pl.when(stays)
    def _():
        arrived(p_in, pg_s)

    @pl.when(jnp.logical_not(stays))
    def _():
        arrived(p_in, pg_s)
        arrived(p_in.at[0], pg_s)

    arrived(f_other, fx_s)
    arrived(h.at[pl.ds(0, TOK)], hx_s)
    h_t[...] = h[pl.ds(0, TOK), :].T

    @pl.when(is_owner)
    def _():
        f_red[...] = add_up(f_part, f_in, f_r)
        hand_round(f_red, f_full, fg_s, fg_r)

    sent(f_in, f_s)
    arrived(c_all.at[pl.ds(0, Z * HALF)], c_r)
    for t in range(Z):
        remote(c_rows(t, core), c_rows(t, core), cf_s, cf_r, dp=sibling).start()
    arrived(f_full, fg_r)

    f2 = split(f_full[...])
    w_part[...] = fold(mm(f2, h_t[...]))

    for half in range(2):
        for t in range(4):
            x = w_part[16 * half : 16 * half + 16, 128 * t : 128 * t + 128]
            w_pack[half, 2 * t], w_pack[half, 2 * t + 1] = interleave(x[:8], x[8:])
    for j, o in enumerate(LINE):
        remote(w_pack.at[core, along(o)], w_in.at[j], w_s, w_r, mp=along(o)).start()
        remote(w_pack.at[1 - core, along(o)], w_in.at[Z - 1 + j], w_s, w_r, dp=sibling, mp=along(o)).start()
    remote(w_pack.at[1 - core, z], w_in.at[2 * Z - 2], w_s, w_r, dp=sibling).start()
    s_part[...] = fold(mm(f2, e[...]))
    remote(s_part.at[other_half, :], s_other, sx_s, sx_r, dp=sibling).start()
    arrived(c_all.at[pl.ds(0, Z * HALF)], cf_r)
    arrived(w_in, w_r)
    total = w_pack[core, z]
    for j in range(Z - 1):
        total += w_in[j]
    other = w_in[Z - 1]
    for j in range(Z, 2 * Z - 1):
        other += w_in[j]
    first, second = replicas(total, other)
    tokens = jnp.concatenate(interleave(first, second), axis=0)
    v = fold(mm_t(split(tokens), c_all[...]))
    arrived(s_other, sx_r)
    s_part[own_half, :] += s_other[...] + v
    to_owners(s_part, s_in, s_s, s_r)
    gram = mm_t(f2, f2)
    g_part[...] = pack(fold(gram[:, :RANK] + gram[:, RANK:]))
    g_sends = [remote(g_part, g_in.at[z], g_s, g_r, mp=along(o)) for j, o in enumerate(LINE)]
    for c in g_sends:
        c.start()
    pltpu.make_async_copy(g_part, g_in.at[z], g_r).start()

    arrived(c_pack.at[pl.ds(0, Z - 1)], c_s)
    arrived(cot_x, cx_s)
    arrived(c_all.at[pl.ds(0, Z * HALF)], cf_s)
    arrived(s_other, sx_s)
    arrived(w_in, w_s)
    arrived(g_in.at[pl.ds(0, Z - 1)], g_s)

    @pl.when(is_owner)
    def _():
        arrived(f_in, fg_s)
        arrived(f_in, fg_s)
        arrived(f_in.at[0], fg_s)

    @pl.when(is_owner)
    def _():
        s_red[...] = add_up(s_part, s_in, s_r)

        for j, o in enumerate(LINE):
            remote(s_red, z_in.at[z], zs_s, zs_r, mp=along(o)).start()
        pltpu.make_async_copy(s_red, z_in.at[z], zs_r).start()

    arrived(g_in, g_r)
    total = g_in[0]
    for j in range(1, Z):
        total += g_in[j]
    inverse = inverse_lower(unpack(total))

    left = left_terms(inverse)
    both[:RANK] = mm(left, right_terms(f_full[...]))

    @pl.when(is_owner)
    def _():
        arrived(z_in, zs_r)
        total = z_in[0]
        for j in range(1, Z):
            total += z_in[j]
        s_tot[...] = total
        hand_round(s_tot, s_full, sg_s, sg_r)
        arrived(z_in.at[pl.ds(0, Z - 1)], zs_s)

    sent(s_in, s_s)
    arrived(s_full, sg_r)
    both[RANK:] = mm(left, right_terms(s_full[...]))

    @pl.when(is_owner)
    def _():
        arrived(s_in, sg_s)
        arrived(s_in, sg_s)
        arrived(s_in.at[0], sg_s)


def shards(hidden, upstream, reward_head, margins, ends, residual_error, previous_q):
    hbm_spec = pl.BlockSpec(memory_space=pltpu.HBM)
    vmem_spec = pl.BlockSpec(memory_space=pltpu.VMEM)
    vmem, dma = pltpu.VMEM, pltpu.SemaphoreType.DMA
    both = pl.pallas_call(
        kernel,
        out_shape=vmem((2 * RANK, D), F32),
        in_specs=[hbm_spec] * 7,
        out_specs=vmem_spec,
        scratch_shapes=[
            vmem((2 * TOK, D), BF16), vmem((D, TOK), BF16), vmem((D, D), BF16), vmem((WIDTH, TOK), BF16), vmem((WIDTH,), F32),
            vmem((1, PAIRS), F32), vmem((2, PAIRS), jnp.int32), vmem((RANK, D), F32), vmem((2 * RANK, D), BF16),
            vmem((CH, TOK), BF16), vmem((HALF, TOK), BF16), vmem((Z, HALF, 128), BF16), vmem((D, 128), BF16),
            vmem((RANK, TOK), F32), vmem((Z - 1, 8, 256), F32), vmem((8, 256), F32), vmem((2, 16, TOK), F32),
            vmem((RANK, D), F32), vmem((16, D), F32), vmem((len(CHIPS), 8, CH), F32), vmem((8, CH), F32),
            vmem((RANK, D), F32),
            vmem((RANK, TOK), F32), vmem((2, Z, 8, 128), F32), vmem((2 * Z - 1, 8, 128), F32),
            vmem((8, 128), F32), vmem((Z, 8, 128), F32),
            vmem((RANK, D), F32), vmem((16, D), F32), vmem((len(CHIPS), 8, CH), F32), vmem((8, CH), F32), vmem((Z, 8, CH), F32), vmem((8, CH), F32), vmem((RANK, D), F32),
            dma((6,)), dma((PARTS,)),
            *[dma(())] * 30,
        ],
        compiler_params=pltpu.CompilerParams(
            collective_id=0, has_side_effects=True, vmem_limit_bytes=48 * 1024 * 1024
        ),
        cost_estimate=pl.CostEstimate(flops=2_000_000_000, bytes_accessed=14_000_000, transcendentals=0),
        name="power_step",
    )(
        *(
            pltpu.with_memory_space_constraint(x, pltpu.HBM)
            for x in (
                hidden, upstream.T, reward_head, margins.reshape(1, PAIRS), ends.T, residual_error, previous_q.T
            )
        )
    )
    return both[:RANK].T * math.sqrt(FF), both[RANK:].T * (1.0 / NDP)


def solution(mesh):
    in_specs = (
        P("dp", "mp"),
        P("dp", "mp"),
        P("mp"),
        P("dp"),
        P("dp", None),
        P("dp", "mp", None),
        P(),
    )
    out_specs = (P("mp", None), P())
    return jax.shard_map(shards, mesh=mesh, in_specs=in_specs, out_specs=out_specs, check_vma=False)
```

```python
import math

import jax
import jax.numpy as jnp
from jax import lax
from jax.experimental import pallas as pl
from jax.experimental.pallas import tpu as pltpu
from jax.sharding import PartitionSpec as P

FF = 18432
D = 2304
RANK = 32
TOK = 512
PAIRS = 16
WIDTH = 288
Z = 8
NDP = 32
HALF = WIDTH // 2
OWNERS = 24
CH = 384
PARTS = 9
PART = D // PARTS
MESH = pl.DeviceIdType.MESH
F32 = jnp.float32
BF16 = jnp.bfloat16


def ring(step, size):
    return min(step, size - step)


PLANE = sorted(
    ((dy, dx, dc) for dy in range(4) for dx in range(4) for dc in range(2) if (dy, dx, dc) != (0, 0, 0)),
    key=lambda o: -(ring(o[0], 4) + ring(o[1], 4)),
)
CHIPS = [o[:2] for o in PLANE if o[2] == 0]
LINE = (4, 3, 5, 2, 6, 1, 7)


def thirds(x):
    high = x.astype(BF16).astype(F32)
    middle = (x - high).astype(BF16).astype(F32)
    return high, middle, (x - high - middle).astype(BF16).astype(F32)


def split(x):
    return jnp.concatenate([t.astype(BF16) for t in thirds(x)], axis=0)


def fold(x):
    rows = x.shape[0] // 3
    return x[:rows] + x[rows : 2 * rows] + x[2 * rows :]


def mm(a, b):
    return lax.dot_general(a, b, (((1,), (0,)), ((), ())), preferred_element_type=F32)


def mm_t(a, b):
    return lax.dot_general(a, b, (((1,), (1,)), ((), ())), preferred_element_type=F32)


def pack(x):
    return jnp.concatenate([x[8 * i : 8 * i + 8] for i in range(4)], axis=1)


def unpack(x):
    return jnp.concatenate([x[:, 32 * i : 32 * i + 32] for i in range(4)], axis=0)


def left_terms(x):
    high, middle, low = thirds(x)
    return jnp.concatenate([high, high, middle, high, middle, low], axis=1).astype(BF16)


def right_terms(x):
    high, middle, low = (t.astype(BF16) for t in thirds(x))
    return jnp.concatenate([high, middle, high, low, middle, high], axis=0)


def interleave(a, b):
    low = lax.broadcasted_iota(jnp.int32, a.shape, 1) < 64
    return jnp.where(low, a, pltpu.roll(b, 64, 1)), jnp.where(low, pltpu.roll(a, 64, 1), b)


def column(row):
    n = row.shape[1]
    same = lax.broadcasted_iota(jnp.int32, (n, n), 0) == lax.broadcasted_iota(jnp.int32, (n, n), 1)
    return jnp.sum(jnp.where(same, jnp.broadcast_to(row, (n, n)), 0.0), axis=1, keepdims=True)


def inverse_lower(gram):
    rows = lax.broadcasted_iota(jnp.int32, (RANK, 128), 0)
    lanes = lax.broadcasted_iota(jnp.int32, (RANK, 128), 1)
    eye = (lanes == rows + RANK).astype(F32)
    m = jnp.concatenate([gram, jnp.zeros((RANK, 128 - RANK), F32)], axis=1) + eye
    for k in range(RANK - 1):
        col = m[:, k : k + 1]
        pivot = m[k : k + 1, :]
        scale = jnp.where(rows[:, :1] > k, col / m[k : k + 1, k : k + 1], 0.0)
        m = m - scale * pivot
    diag = jnp.sum(jnp.where(lanes == rows, m, 0.0), axis=1, keepdims=True)
    return (m * lax.rsqrt(diag))[:, RANK : 2 * RANK]


def kernel(
    hidden, upstream_t, head, margins, ends_t, error, q_t,
    both,
    h, h_t, e, u, hd, mg, en, q, q2, cot, cot_x, c_pack, c_all,
    p_part, p_in, p_red, p_full,
    f_part, f_other, f_in, f_red, f_full,
    w_part, w_pack, w_in, g_part, g_in,
    s_part, s_other, s_in, s_red, z_in, s_tot, s_full,
    load, e_load,
    p_s, p_r, pg_s, pg_r, c_s, c_r, f_s, f_r, fg_s, fg_r,
    w_s, w_r, g_s, g_r, s_s, s_r, zs_s, zs_r, sg_s, sg_r,
    hx_s, hx_r, fx_s, fx_r, cx_s, cx_r, cf_s, cf_r, sx_s, sx_r,
):
    dp, z = lax.axis_index("dp"), lax.axis_index("mp")
    core, chip = lax.rem(dp, 2), lax.div(dp, 2)
    cy, cx = lax.div(chip, 4), lax.rem(chip, 4)

    def place(y, x):
        return lax.rem(x + y + 2 * core, 4)

    def chunk(ref, y, x):
        k = 3 * y + place(y, x) - 1
        row = pl.multiple_of(16 * core + lax.div(k, 6) * 8, 8)
        lane = pl.multiple_of(lax.rem(k, 6) * CH, 128)
        return ref.at[pl.ds(row, 8), pl.ds(lane, CH)]

    def away(o):
        dy, dx, dc = o
        return lax.rem(cy + dy, 4), lax.rem(cx + dx, 4), lax.rem(core + dc, 2)

    def along(step):
        return lax.rem(z + step, Z)

    is_owner = place(cy, cx) != 0
    own_half = pl.ds(pl.multiple_of(16 * core, 16), 16)
    other_half = pl.ds(pl.multiple_of(16 * (1 - core), 16), 16)
    sibling = dp + 1 - 2 * core

    def remote(src, dst, send, recv, **to):
        return pltpu.make_async_remote_copy(
            src_ref=src, dst_ref=dst, send_sem=send, recv_sem=recv, device_id=to, device_id_type=MESH
        )

    def arrived(ref, sem):
        pltpu.make_async_copy(ref, ref, sem).wait()

    loads = [
        pltpu.make_async_copy(src, dst, load.at[i])
        for i, (src, dst) in enumerate(
            [(upstream_t, u), (margins, mg), (ends_t, en), (head, hd), (q_t, q), (hidden, h.at[pl.ds(0, TOK)])]
        )
    ]
    e_loads = [
        pltpu.make_async_copy(error.at[0, pl.ds(PART * i, PART)], e.at[pl.ds(PART * i, PART)], e_load.at[i])
        for i in range(PARTS)
    ]
    for c in loads[:5]:
        c.start()

    barrier = pltpu.get_barrier_semaphore()
    for step in LINE:
        pl.semaphore_signal(barrier, inc=1, device_id={"mp": along(step)}, device_id_type=MESH)
        pl.semaphore_signal(barrier, inc=1, device_id={"dp": sibling, "mp": along(step)}, device_id_type=MESH)
    for o in PLANE:
        y, x, c = away(o)
        pl.semaphore_signal(barrier, inc=1, device_id={"dp": (y * 4 + x) * 2 + c}, device_id_type=MESH)
    for c in e_loads + loads[5:]:
        c.start()

    shift = pl.multiple_of(lax.rem(z, 4) * 32, 32)
    window = pl.multiple_of((2 * z + lax.div(z, 4)) * 128, 128)
    cot[...] = jnp.zeros_like(cot)
    for c in loads[:5]:
        c.wait()
    push = jax.nn.sigmoid(-column(mg[...]))
    spots = en[...].astype(F32)
    places = lax.broadcasted_iota(jnp.int32, (PAIRS, TOK), 1).astype(F32)
    weight = jnp.sum(
        jnp.where(places == column(spots[1:2]), push, 0.0) - jnp.where(places == column(spots[0:1]), push, 0.0),
        axis=0,
        keepdims=True,
    )
    direction = jnp.broadcast_to(hd[...].reshape(1, WIDTH), (128, WIDTH)).T[:, :1]
    cot[pl.ds(shift, WIDTH), :] = (u[...].astype(F32) + direction * weight).astype(BF16)
    q2[...] = split(q[...])
    p_part[...] = fold(mm(q2[:, pl.ds(window, CH)], cot[...]))
    pl.semaphore_wait(barrier, NDP - 1 + 2 * (Z - 1))

    def replicas(mine, other):
        return jnp.where(core == 0, mine, other), jnp.where(core == 0, other, mine)

    def p_chunk(ref, t):
        row = pl.multiple_of(lax.div(t, 2) * 8, 8)
        return ref.at[pl.ds(row, 8), pl.ds(pl.multiple_of(lax.rem(t, 2) * 256, 128), 256)]

    p_sends = [
        remote(p_chunk(p_part, along(o)), p_in.at[j], p_s, p_r, mp=along(o)) for j, o in enumerate(LINE)
    ]
    for c in p_sends:
        c.start()
    def c_half(c):
        return cot.at[pl.ds(pl.multiple_of(shift + HALF * c, 16), HALF), :]

    remote(c_half(1 - core), cot_x, cx_s, cx_r, dp=sibling).start()
    remote(hidden, h.at[pl.ds(TOK, TOK)], hx_s, hx_r, dp=sibling).start()
    def error_part(first, last):
        for i in range(first, last):
            e_loads[i].wait()
            f_part[:, PART * i : PART * (i + 1)] = fold(mm_t(q2[...], e[PART * i : PART * (i + 1), :]))

    error_part(0, 5)
    arrived(p_in, p_r)
    total = p_chunk(p_part, z)[...]
    for j in range(Z - 1):
        total += p_in[j]
    p_red[...] = total
    def p_place(slot):
        row = pl.multiple_of(lax.rem(lax.div(z, 2), 2) * 8, 8)
        return p_full.at[slot, pl.ds(row, 8), pl.ds(pl.multiple_of(lax.rem(z, 2) * 256, 128), 256)]

    stays = lax.div(z, 4) == core

    @pl.when(stays)
    def _():
        for o in LINE:
            remote(p_red, p_place(0), pg_s, pg_r, mp=along(o)).start()
        pltpu.make_async_copy(p_red, p_place(0), pg_r).start()

    @pl.when(jnp.logical_not(stays))
    def _():
        for o in LINE:
            remote(p_red, p_place(1), pg_s, pg_r, dp=sibling, mp=along(o)).start()
        remote(p_red, p_place(1), pg_s, pg_r, dp=sibling).start()

    def c_rows(t, c):
        return c_all.at[pl.ds(pl.multiple_of(t * WIDTH + c * HALF, 16), HALF)]

    error_part(5, PARTS)
    remote(f_part.at[other_half, :], f_other, fx_s, fx_r, dp=sibling).start()
    arrived(cot_x, cx_r)
    first, second = replicas(c_half(core)[...].astype(F32), cot_x[...].astype(F32))
    for t in range(4):
        even, odd = interleave(first[:, 128 * t : 128 * t + 128], second[:, 128 * t : 128 * t + 128])
        c_pack[2 * t] = even.astype(BF16)
        c_pack[2 * t + 1] = odd.astype(BF16)
    loads[5].wait()
    arrived(p_in, p_s)
    arrived(h.at[pl.ds(TOK, TOK)], hx_r)
    arrived(f_other, fx_r)
    arrived(p_full, pg_r)
    probe = jnp.concatenate([p_full[0], p_full[1]], axis=1)
    f_part[own_half, :] += f_other[...] + fold(mm(split(probe), h[...]))

    def to_owners(part, into, send, recv):
        for j, (dy, dx) in enumerate(CHIPS):
            y, x = lax.rem(cy + dy, 4), lax.rem(cx + dx, 4)

            @pl.when(place(y, x) != 0)
            def _(j=j, y=y, x=x):
                remote(chunk(part, y, x), into.at[j], send, recv, dp=y * 8 + x * 2 + core).start()

    def sent(into, send):
        @pl.when(is_owner)
        def _():
            arrived(into.at[pl.ds(0, OWNERS // 2 - 1)], send)

        @pl.when(jnp.logical_not(is_owner))
        def _():
            arrived(into.at[pl.ds(0, OWNERS // 2)], send)

    def add_up(part, into, recv):
        arrived(into, recv)
        total = chunk(part, cy, cx)[...]
        for j in range(len(CHIPS)):
            total += into[j]
        return total

    def hand_round(red, full, send, recv):
        for o in PLANE:
            y, x, c = away(o)
            remote(red, chunk(full, cy, cx), send, recv, dp=(y * 4 + x) * 2 + c).start()
        pltpu.make_async_copy(red, chunk(full, cy, cx), recv).start()

    to_owners(f_part, f_in, f_s, f_r)
    for o in LINE:
        remote(c_pack.at[along(o)], c_rows(z, core), c_s, c_r, mp=along(o)).start()
    pltpu.make_async_copy(c_pack.at[z], c_rows(z, core), c_r).start()
    @pl.when(stays)
    def _():
        arrived(p_in, pg_s)

    @pl.when(jnp.logical_not(stays))
    def _():
        arrived(p_in, pg_s)
        arrived(p_in.at[0], pg_s)

    arrived(f_other, fx_s)
    arrived(h.at[pl.ds(0, TOK)], hx_s)
    h_t[...] = h[pl.ds(0, TOK), :].T

    @pl.when(is_owner)
    def _():
        f_red[...] = add_up(f_part, f_in, f_r)
        hand_round(f_red, f_full, fg_s, fg_r)

    sent(f_in, f_s)
    arrived(c_all.at[pl.ds(0, Z * HALF)], c_r)
    for t in range(Z):
        remote(c_rows(t, core), c_rows(t, core), cf_s, cf_r, dp=sibling).start()
    arrived(f_full, fg_r)

    f2 = split(f_full[...])
    w_part[...] = fold(mm(f2, h_t[...]))

    for half in range(2):
        for t in range(4):
            x = w_part[16 * half : 16 * half + 16, 128 * t : 128 * t + 128]
            w_pack[half, 2 * t], w_pack[half, 2 * t + 1] = interleave(x[:8], x[8:])
    for j, o in enumerate(LINE):
        remote(w_pack.at[core, along(o)], w_in.at[j], w_s, w_r, mp=along(o)).start()
        remote(w_pack.at[1 - core, along(o)], w_in.at[Z - 1 + j], w_s, w_r, dp=sibling, mp=along(o)).start()
    remote(w_pack.at[1 - core, z], w_in.at[2 * Z - 2], w_s, w_r, dp=sibling).start()
    s_part[...] = fold(mm(f2, e[...]))
    remote(s_part.at[other_half, :], s_other, sx_s, sx_r, dp=sibling).start()
    arrived(c_all.at[pl.ds(0, Z * HALF)], cf_r)
    arrived(w_in, w_r)
    total = w_pack[core, z]
    for j in range(Z - 1):
        total += w_in[j]
    other = w_in[Z - 1]
    for j in range(Z, 2 * Z - 1):
        other += w_in[j]
    first, second = replicas(total, other)
    tokens = jnp.concatenate(interleave(first, second), axis=0)
    v = fold(mm_t(split(tokens), c_all[...]))
    arrived(s_other, sx_r)
    s_part[own_half, :] += s_other[...] + v
    to_owners(s_part, s_in, s_s, s_r)
    gram = mm_t(f2, f2)
    g_part[...] = pack(fold(gram[:, :RANK] + gram[:, RANK : 2 * RANK] + gram[:, 2 * RANK :]))
    g_sends = [remote(g_part, g_in.at[z], g_s, g_r, mp=along(o)) for j, o in enumerate(LINE)]
    for c in g_sends:
        c.start()
    pltpu.make_async_copy(g_part, g_in.at[z], g_r).start()

    arrived(c_pack.at[pl.ds(0, Z - 1)], c_s)
    arrived(cot_x, cx_s)
    arrived(c_all.at[pl.ds(0, Z * HALF)], cf_s)
    arrived(s_other, sx_s)
    arrived(w_in, w_s)
    arrived(g_in.at[pl.ds(0, Z - 1)], g_s)

    @pl.when(is_owner)
    def _():
        arrived(f_in, fg_s)
        arrived(f_in, fg_s)
        arrived(f_in.at[0], fg_s)

    @pl.when(is_owner)
    def _():
        s_red[...] = add_up(s_part, s_in, s_r)

        for j, o in enumerate(LINE):
            remote(s_red, z_in.at[z], zs_s, zs_r, mp=along(o)).start()
        pltpu.make_async_copy(s_red, z_in.at[z], zs_r).start()

    arrived(g_in, g_r)
    total = g_in[0]
    for j in range(1, Z):
        total += g_in[j]
    inverse = inverse_lower(unpack(total))

    left = left_terms(inverse)
    both[:RANK] = mm(left, right_terms(f_full[...]))

    @pl.when(is_owner)
    def _():
        arrived(z_in, zs_r)
        total = z_in[0]
        for j in range(1, Z):
            total += z_in[j]
        s_tot[...] = total
        hand_round(s_tot, s_full, sg_s, sg_r)
        arrived(z_in.at[pl.ds(0, Z - 1)], zs_s)

    sent(s_in, s_s)
    arrived(s_full, sg_r)
    both[RANK:] = mm(left, right_terms(s_full[...]))

    @pl.when(is_owner)
    def _():
        arrived(s_in, sg_s)
        arrived(s_in, sg_s)
        arrived(s_in.at[0], sg_s)


def shards(hidden, upstream, reward_head, margins, ends, residual_error, previous_q):
    hbm_spec = pl.BlockSpec(memory_space=pltpu.HBM)
    vmem_spec = pl.BlockSpec(memory_space=pltpu.VMEM)
    vmem, dma = pltpu.VMEM, pltpu.SemaphoreType.DMA
    both = pl.pallas_call(
        kernel,
        out_shape=vmem((2 * RANK, D), F32),
        in_specs=[hbm_spec] * 7,
        out_specs=vmem_spec,
        scratch_shapes=[
            vmem((2 * TOK, D), BF16), vmem((D, TOK), BF16), vmem((D, D), BF16), vmem((WIDTH, TOK), BF16), vmem((WIDTH,), F32),
            vmem((1, PAIRS), F32), vmem((2, PAIRS), jnp.int32), vmem((RANK, D), F32), vmem((3 * RANK, D), BF16),
            vmem((CH, TOK), BF16), vmem((HALF, TOK), BF16), vmem((Z, HALF, 128), BF16), vmem((D, 128), BF16),
            vmem((RANK, TOK), F32), vmem((Z - 1, 8, 256), F32), vmem((8, 256), F32), vmem((2, 16, TOK), F32),
            vmem((RANK, D), F32), vmem((16, D), F32), vmem((len(CHIPS), 8, CH), F32), vmem((8, CH), F32),
            vmem((RANK, D), F32),
            vmem((RANK, TOK), F32), vmem((2, Z, 8, 128), F32), vmem((2 * Z - 1, 8, 128), F32),
            vmem((8, 128), F32), vmem((Z, 8, 128), F32),
            vmem((RANK, D), F32), vmem((16, D), F32), vmem((len(CHIPS), 8, CH), F32), vmem((8, CH), F32), vmem((Z, 8, CH), F32), vmem((8, CH), F32), vmem((RANK, D), F32),
            dma((6,)), dma((PARTS,)),
            *[dma(())] * 30,
        ],
        compiler_params=pltpu.CompilerParams(
            collective_id=0, has_side_effects=True, vmem_limit_bytes=48 * 1024 * 1024
        ),
        cost_estimate=pl.CostEstimate(flops=2_000_000_000, bytes_accessed=14_000_000, transcendentals=0),
        name="power_step",
    )(
        *(
            pltpu.with_memory_space_constraint(x, pltpu.HBM)
            for x in (
                hidden, upstream.T, reward_head, margins.reshape(1, PAIRS), ends.T, residual_error, previous_q.T
            )
        )
    )
    return both[:RANK].T * math.sqrt(FF), both[RANK:].T * (1.0 / NDP)


def solution(mesh):
    in_specs = (
        P("dp", "mp"),
        P("dp", "mp"),
        P("mp"),
        P("dp"),
        P("dp", None),
        P("dp", "mp", None),
        P(),
    )
    out_specs = (P("mp", None), P())
    return jax.shard_map(shards, mesh=mesh, in_specs=in_specs, out_specs=out_specs, check_vma=False)
```

```python
import math

import jax
import jax.numpy as jnp
from jax import lax
from jax.experimental import pallas as pl
from jax.experimental.pallas import tpu as pltpu
from jax.sharding import PartitionSpec as P

FF = 18432
D = 2304
RANK = 32
TOK = 512
PAIRS = 16
WIDTH = 288
Z = 8
NDP = 32
HALF = WIDTH // 2
OWNERS = 24
CH = 384
PARTS = 9
PART = D // PARTS
MESH = pl.DeviceIdType.MESH
F32 = jnp.float32
BF16 = jnp.bfloat16


def ring(step, size):
    return min(step, size - step)


PLANE = sorted(
    ((dy, dx, dc) for dy in range(4) for dx in range(4) for dc in range(2) if (dy, dx, dc) != (0, 0, 0)),
    key=lambda o: -(ring(o[0], 4) + ring(o[1], 4)),
)
CHIPS = [o[:2] for o in PLANE if o[2] == 0]
LINE = (4, 3, 5, 2, 6, 1, 7)


def thirds(x):
    high = x.astype(BF16).astype(F32)
    middle = (x - high).astype(BF16).astype(F32)
    return high, middle, (x - high - middle).astype(BF16).astype(F32)


def split(x):
    return jnp.concatenate([t.astype(BF16) for t in thirds(x)], axis=0)


def fold(x):
    rows = x.shape[0] // 3
    return x[:rows] + x[rows : 2 * rows] + x[2 * rows :]


def mm(a, b):
    return lax.dot_general(a, b, (((1,), (0,)), ((), ())), preferred_element_type=F32)


def mm_t(a, b):
    return lax.dot_general(a, b, (((1,), (1,)), ((), ())), preferred_element_type=F32)


def pack(x):
    return jnp.concatenate([x[8 * i : 8 * i + 8] for i in range(4)], axis=1)


def unpack(x):
    return jnp.concatenate([x[:, 32 * i : 32 * i + 32] for i in range(4)], axis=0)


def left_terms(x):
    high, middle, low = thirds(x)
    return jnp.concatenate([high, high, middle, high, middle, low], axis=1).astype(BF16)


def right_terms(x):
    high, middle, low = (t.astype(BF16) for t in thirds(x))
    return jnp.concatenate([high, middle, high, low, middle, high], axis=0)


def interleave(a, b):
    low = lax.broadcasted_iota(jnp.int32, a.shape, 1) < 64
    return jnp.where(low, a, pltpu.roll(b, 64, 1)), jnp.where(low, pltpu.roll(a, 64, 1), b)


def column(row):
    n = row.shape[1]
    same = lax.broadcasted_iota(jnp.int32, (n, n), 0) == lax.broadcasted_iota(jnp.int32, (n, n), 1)
    return jnp.sum(jnp.where(same, jnp.broadcast_to(row, (n, n)), 0.0), axis=1, keepdims=True)


def inverse_lower(gram):
    rows = lax.broadcasted_iota(jnp.int32, (RANK, 128), 0)
    lanes = lax.broadcasted_iota(jnp.int32, (RANK, 128), 1)
    eye = (lanes == rows + RANK).astype(F32)
    m = jnp.concatenate([gram, jnp.zeros((RANK, 128 - RANK), F32)], axis=1) + eye
    for k in range(RANK - 1):
        col = m[:, k : k + 1]
        pivot = m[k : k + 1, :]
        scale = jnp.where(rows[:, :1] > k, col / m[k : k + 1, k : k + 1], 0.0)
        m = m - scale * pivot
    diag = jnp.sum(jnp.where(lanes == rows, m, 0.0), axis=1, keepdims=True)
    return (m * lax.rsqrt(diag))[:, RANK : 2 * RANK]


def kernel(
    hidden, upstream_t, head, margins, ends_t, error, q_t,
    both,
    h, h_t, e, u, hd, mg, en, q, q2, cot, cot_x, c_pack, c_all,
    p_part, p_in, p_red, p_full,
    f_part, f_other, f_in, f_red, f_full,
    w_part, w_pack, w_in, g_part, g_in,
    s_part, s_other, s_in, s_red, z_in, s_tot, s_full,
    load, e_load,
    p_s, p_r, pg_s, pg_r, c_s, c_r, f_s, f_r, fg_s, fg_r,
    w_s, w_r, g_s, g_r, s_s, s_r, zs_s, zs_r, sg_s, sg_r,
    hx_s, hx_r, fx_s, fx_r, cx_s, cx_r, cf_s, cf_r, sx_s, sx_r,
):
    dp, z = lax.axis_index("dp"), lax.axis_index("mp")
    core, chip = lax.rem(dp, 2), lax.div(dp, 2)
    cy, cx = lax.div(chip, 4), lax.rem(chip, 4)

    def place(y, x):
        return lax.rem(x + y + 2 * core, 4)

    def chunk(ref, y, x):
        k = 3 * y + place(y, x) - 1
        row = pl.multiple_of(16 * core + lax.div(k, 6) * 8, 8)
        lane = pl.multiple_of(lax.rem(k, 6) * CH, 128)
        return ref.at[pl.ds(row, 8), pl.ds(lane, CH)]

    def away(o):
        dy, dx, dc = o
        return lax.rem(cy + dy, 4), lax.rem(cx + dx, 4), lax.rem(core + dc, 2)

    def along(step):
        return lax.rem(z + step, Z)

    is_owner = place(cy, cx) != 0
    own_half = pl.ds(pl.multiple_of(16 * core, 16), 16)
    other_half = pl.ds(pl.multiple_of(16 * (1 - core), 16), 16)
    sibling = dp + 1 - 2 * core

    def remote(src, dst, send, recv, **to):
        return pltpu.make_async_remote_copy(
            src_ref=src, dst_ref=dst, send_sem=send, recv_sem=recv, device_id=to, device_id_type=MESH
        )

    def arrived(ref, sem):
        pltpu.make_async_copy(ref, ref, sem).wait()

    loads = [
        pltpu.make_async_copy(src, dst, load.at[i])
        for i, (src, dst) in enumerate(
            [(upstream_t, u), (margins, mg), (ends_t, en), (head, hd), (q_t, q), (hidden, h.at[pl.ds(0, TOK)])]
        )
    ]
    e_loads = [
        pltpu.make_async_copy(error.at[0, pl.ds(PART * i, PART)], e.at[pl.ds(PART * i, PART)], e_load.at[i])
        for i in range(PARTS)
    ]
    barrier = pltpu.get_barrier_semaphore()
    for step in LINE:
        pl.semaphore_signal(barrier, inc=1, device_id={"mp": along(step)}, device_id_type=MESH)
        pl.semaphore_signal(barrier, inc=1, device_id={"dp": sibling, "mp": along(step)}, device_id_type=MESH)
    for o in PLANE:
        y, x, c = away(o)
        pl.semaphore_signal(barrier, inc=1, device_id={"dp": (y * 4 + x) * 2 + c}, device_id_type=MESH)
    for c in loads[:5] + e_loads + loads[5:]:
        c.start()

    shift = pl.multiple_of(lax.rem(z, 4) * 32, 32)
    window = pl.multiple_of((2 * z + lax.div(z, 4)) * 128, 128)
    cot[...] = jnp.zeros_like(cot)
    for c in loads[:5]:
        c.wait()
    push = jax.nn.sigmoid(-column(mg[...]))
    spots = en[...].astype(F32)
    places = lax.broadcasted_iota(jnp.int32, (PAIRS, TOK), 1).astype(F32)
    weight = jnp.sum(
        jnp.where(places == column(spots[1:2]), push, 0.0) - jnp.where(places == column(spots[0:1]), push, 0.0),
        axis=0,
        keepdims=True,
    )
    direction = jnp.broadcast_to(hd[...].reshape(1, WIDTH), (128, WIDTH)).T[:, :1]
    cot[pl.ds(shift, WIDTH), :] = (u[...].astype(F32) + direction * weight).astype(BF16)
    q2[...] = split(q[...])
    p_part[...] = fold(mm(q2[:, pl.ds(window, CH)], cot[...]))
    pl.semaphore_wait(barrier, NDP - 1 + 2 * (Z - 1))

    def replicas(mine, other):
        return jnp.where(core == 0, mine, other), jnp.where(core == 0, other, mine)

    def p_chunk(ref, t):
        row = pl.multiple_of(lax.div(t, 2) * 8, 8)
        return ref.at[pl.ds(row, 8), pl.ds(pl.multiple_of(lax.rem(t, 2) * 256, 128), 256)]

    p_sends = [
        remote(p_chunk(p_part, along(o)), p_in.at[j], p_s, p_r, mp=along(o)) for j, o in enumerate(LINE)
    ]
    for c in p_sends:
        c.start()
    def c_half(c):
        return cot.at[pl.ds(pl.multiple_of(shift + HALF * c, 16), HALF), :]

    remote(c_half(1 - core), cot_x, cx_s, cx_r, dp=sibling).start()
    remote(hidden, h.at[pl.ds(TOK, TOK)], hx_s, hx_r, dp=sibling).start()
    def error_part(first, last):
        for i in range(first, last):
            e_loads[i].wait()
            f_part[:, PART * i : PART * (i + 1)] = fold(mm_t(q2[...], e[PART * i : PART * (i + 1), :]))

    error_part(0, 5)
    early, late = pl.ds(0, 5 * PART), pl.ds(5 * PART, 4 * PART)
    remote(f_part.at[other_half, early], f_other.at[:, early], fx_s, fx_r, dp=sibling).start()
    arrived(p_in, p_r)
    total = p_chunk(p_part, z)[...]
    for j in range(Z - 1):
        total += p_in[j]
    p_red[...] = total
    def p_place(slot):
        row = pl.multiple_of(lax.rem(lax.div(z, 2), 2) * 8, 8)
        return p_full.at[slot, pl.ds(row, 8), pl.ds(pl.multiple_of(lax.rem(z, 2) * 256, 128), 256)]

    stays = lax.div(z, 4) == core

    @pl.when(stays)
    def _():
        for o in LINE:
            remote(p_red, p_place(0), pg_s, pg_r, mp=along(o)).start()
        pltpu.make_async_copy(p_red, p_place(0), pg_r).start()

    @pl.when(jnp.logical_not(stays))
    def _():
        for o in LINE:
            remote(p_red, p_place(1), pg_s, pg_r, dp=sibling, mp=along(o)).start()
        remote(p_red, p_place(1), pg_s, pg_r, dp=sibling).start()

    def c_rows(t, c):
        return c_all.at[pl.ds(pl.multiple_of(t * WIDTH + c * HALF, 16), HALF)]

    error_part(5, PARTS)
    remote(f_part.at[other_half, late], f_other.at[:, late], fx_s, fx_r, dp=sibling).start()
    arrived(cot_x, cx_r)
    first, second = replicas(c_half(core)[...].astype(F32), cot_x[...].astype(F32))
    for t in range(4):
        even, odd = interleave(first[:, 128 * t : 128 * t + 128], second[:, 128 * t : 128 * t + 128])
        c_pack[2 * t] = even.astype(BF16)
        c_pack[2 * t + 1] = odd.astype(BF16)
    loads[5].wait()
    arrived(p_in, p_s)
    arrived(h.at[pl.ds(TOK, TOK)], hx_r)
    arrived(p_full, pg_r)
    probe = jnp.concatenate([p_full[0], p_full[1]], axis=1)
    leading = fold(mm(split(probe), h[...]))
    arrived(f_other, fx_r)
    f_part[own_half, :] += f_other[...] + leading

    def to_owners(part, into, send, recv):
        for j, (dy, dx) in enumerate(CHIPS):
            y, x = lax.rem(cy + dy, 4), lax.rem(cx + dx, 4)

            @pl.when(place(y, x) != 0)
            def _(j=j, y=y, x=x):
                remote(chunk(part, y, x), into.at[j], send, recv, dp=y * 8 + x * 2 + core).start()

    def sent(into, send):
        @pl.when(is_owner)
        def _():
            arrived(into.at[pl.ds(0, OWNERS // 2 - 1)], send)

        @pl.when(jnp.logical_not(is_owner))
        def _():
            arrived(into.at[pl.ds(0, OWNERS // 2)], send)

    def add_up(part, into, recv):
        arrived(into, recv)
        total = chunk(part, cy, cx)[...]
        for j in range(len(CHIPS)):
            total += into[j]
        return total

    def hand_round(red, full, send, recv):
        for o in PLANE:
            y, x, c = away(o)
            remote(red, chunk(full, cy, cx), send, recv, dp=(y * 4 + x) * 2 + c).start()
        pltpu.make_async_copy(red, chunk(full, cy, cx), recv).start()

    to_owners(f_part, f_in, f_s, f_r)
    for o in LINE:
        remote(c_pack.at[along(o)], c_rows(z, core), c_s, c_r, mp=along(o)).start()
    pltpu.make_async_copy(c_pack.at[z], c_rows(z, core), c_r).start()
    @pl.when(stays)
    def _():
        arrived(p_in, pg_s)

    @pl.when(jnp.logical_not(stays))
    def _():
        arrived(p_in, pg_s)
        arrived(p_in.at[0], pg_s)

    arrived(f_other, fx_s)
    arrived(h.at[pl.ds(0, TOK)], hx_s)
    h_t[...] = h[pl.ds(0, TOK), :].T

    @pl.when(is_owner)
    def _():
        f_red[...] = add_up(f_part, f_in, f_r)
        hand_round(f_red, f_full, fg_s, fg_r)

    sent(f_in, f_s)
    arrived(c_all.at[pl.ds(0, Z * HALF)], c_r)
    for t in range(Z):
        remote(c_rows(t, core), c_rows(t, core), cf_s, cf_r, dp=sibling).start()
    arrived(f_full, fg_r)

    f2 = split(f_full[...])
    w_part[...] = fold(mm(f2, h_t[...]))

    for half in range(2):
        for t in range(4):
            x = w_part[16 * half : 16 * half + 16, 128 * t : 128 * t + 128]
            w_pack[half, 2 * t], w_pack[half, 2 * t + 1] = interleave(x[:8], x[8:])
    for j, o in enumerate(LINE):
        remote(w_pack.at[core, along(o)], w_in.at[j], w_s, w_r, mp=along(o)).start()
        remote(w_pack.at[1 - core, along(o)], w_in.at[Z - 1 + j], w_s, w_r, dp=sibling, mp=along(o)).start()
    remote(w_pack.at[1 - core, z], w_in.at[2 * Z - 2], w_s, w_r, dp=sibling).start()
    s_part[...] = fold(mm(f2, e[...]))
    remote(s_part.at[other_half, :], s_other, sx_s, sx_r, dp=sibling).start()
    arrived(c_all.at[pl.ds(0, Z * HALF)], cf_r)
    arrived(w_in, w_r)
    total = w_pack[core, z]
    for j in range(Z - 1):
        total += w_in[j]
    other = w_in[Z - 1]
    for j in range(Z, 2 * Z - 1):
        other += w_in[j]
    first, second = replicas(total, other)
    tokens = jnp.concatenate(interleave(first, second), axis=0)
    v = fold(mm_t(split(tokens), c_all[...]))
    arrived(s_other, sx_r)
    s_part[own_half, :] += s_other[...] + v
    to_owners(s_part, s_in, s_s, s_r)
    gram = mm_t(f2, f2)
    g_part[...] = pack(fold(gram[:, :RANK] + gram[:, RANK : 2 * RANK] + gram[:, 2 * RANK :]))
    g_sends = [remote(g_part, g_in.at[z], g_s, g_r, mp=along(o)) for j, o in enumerate(LINE)]
    for c in g_sends:
        c.start()
    pltpu.make_async_copy(g_part, g_in.at[z], g_r).start()

    arrived(c_pack.at[pl.ds(0, Z - 1)], c_s)
    arrived(cot_x, cx_s)
    arrived(c_all.at[pl.ds(0, Z * HALF)], cf_s)
    arrived(s_other, sx_s)
    arrived(w_in, w_s)
    arrived(g_in.at[pl.ds(0, Z - 1)], g_s)

    @pl.when(is_owner)
    def _():
        arrived(f_in, fg_s)
        arrived(f_in, fg_s)
        arrived(f_in.at[0], fg_s)

    @pl.when(is_owner)
    def _():
        s_red[...] = add_up(s_part, s_in, s_r)

        for j, o in enumerate(LINE):
            remote(s_red, z_in.at[z], zs_s, zs_r, mp=along(o)).start()
        pltpu.make_async_copy(s_red, z_in.at[z], zs_r).start()

    arrived(g_in, g_r)
    total = g_in[0]
    for j in range(1, Z):
        total += g_in[j]
    inverse = inverse_lower(unpack(total))

    left = left_terms(inverse)
    both[:RANK] = mm(left, right_terms(f_full[...]))

    @pl.when(is_owner)
    def _():
        arrived(z_in, zs_r)
        total = z_in[0]
        for j in range(1, Z):
            total += z_in[j]
        s_tot[...] = total
        hand_round(s_tot, s_full, sg_s, sg_r)
        arrived(z_in.at[pl.ds(0, Z - 1)], zs_s)

    sent(s_in, s_s)
    arrived(s_full, sg_r)
    both[RANK:] = mm(left, right_terms(s_full[...]))

    @pl.when(is_owner)
    def _():
        arrived(s_in, sg_s)
        arrived(s_in, sg_s)
        arrived(s_in.at[0], sg_s)


def shards(hidden, upstream, reward_head, margins, ends, residual_error, previous_q):
    hbm_spec = pl.BlockSpec(memory_space=pltpu.HBM)
    vmem_spec = pl.BlockSpec(memory_space=pltpu.VMEM)
    vmem, dma = pltpu.VMEM, pltpu.SemaphoreType.DMA
    both = pl.pallas_call(
        kernel,
        out_shape=vmem((2 * RANK, D), F32),
        in_specs=[hbm_spec] * 7,
        out_specs=vmem_spec,
        scratch_shapes=[
            vmem((2 * TOK, D), BF16), vmem((D, TOK), BF16), vmem((D, D), BF16), vmem((WIDTH, TOK), BF16), vmem((WIDTH,), F32),
            vmem((1, PAIRS), F32), vmem((2, PAIRS), jnp.int32), vmem((RANK, D), F32), vmem((3 * RANK, D), BF16),
            vmem((CH, TOK), BF16), vmem((HALF, TOK), BF16), vmem((Z, HALF, 128), BF16), vmem((D, 128), BF16),
            vmem((RANK, TOK), F32), vmem((Z - 1, 8, 256), F32), vmem((8, 256), F32), vmem((2, 16, TOK), F32),
            vmem((RANK, D), F32), vmem((16, D), F32), vmem((len(CHIPS), 8, CH), F32), vmem((8, CH), F32),
            vmem((RANK, D), F32),
            vmem((RANK, TOK), F32), vmem((2, Z, 8, 128), F32), vmem((2 * Z - 1, 8, 128), F32),
            vmem((8, 128), F32), vmem((Z, 8, 128), F32),
            vmem((RANK, D), F32), vmem((16, D), F32), vmem((len(CHIPS), 8, CH), F32), vmem((8, CH), F32), vmem((Z, 8, CH), F32), vmem((8, CH), F32), vmem((RANK, D), F32),
            dma((6,)), dma((PARTS,)),
            *[dma(())] * 30,
        ],
        compiler_params=pltpu.CompilerParams(
            collective_id=0, has_side_effects=True, vmem_limit_bytes=48 * 1024 * 1024
        ),
        cost_estimate=pl.CostEstimate(flops=2_000_000_000, bytes_accessed=14_000_000, transcendentals=0),
        name="power_step",
    )(
        *(
            pltpu.with_memory_space_constraint(x, pltpu.HBM)
            for x in (
                hidden, upstream.T, reward_head, margins.reshape(1, PAIRS), ends.T, residual_error, previous_q.T
            )
        )
    )
    return both[:RANK].T * math.sqrt(FF), both[RANK:].T * (1.0 / NDP)


def solution(mesh):
    in_specs = (
        P("dp", "mp"),
        P("dp", "mp"),
        P("mp"),
        P("dp"),
        P("dp", None),
        P("dp", "mp", None),
        P(),
    )
    out_specs = (P("mp", None), P())
    return jax.shard_map(shards, mesh=mesh, in_specs=in_specs, out_specs=out_specs, check_vma=False)
```
